256 devices in a mesh: seq: 32 (over x, z), head: 8 (over y, core).
Axes of the slice: x: 4, y: 4, z: 8, core: 2. Of those that a mesh axis runs over, the one named last changes fastest.
Arguments:
- queries: bfloat16 [16384, 16, 128], P(('seq', 'head')), may hold values from -6 to 6
- key_vectors: bfloat16 [16384, 16, 128], P(('seq', 'head')), may hold values from -6 to 6
- value_vectors: bfloat16 [16384, 32, 128], P(('seq', 'head')), may hold values from -6 to 6
- output_gate: bfloat16 [16384, 32, 128], P(('seq', 'head')), may hold values from -6 to 6
- write_strength: bfloat16 [16384, 32], P(('seq', 'head'))
- norm_gain: bfloat16 [128], replicated, may hold values from 0.099609375 to 1.8984375
- output_weight: bfloat16 [4096, 2048], P('head'), may hold values from -0.09375 to 0.09375
Outputs:
- projected: bfloat16 [16384, 2048], P(('seq', 'head'))
The draws below stay inside these ranges and needn't reach their ends.
All inputs are finite; a program needn't handle non-finite values.
Results may differ from the reference program's by a relative error of at most 0.017.
Values may be sent and summed in bfloat16 or wider, within the bound.
A program may use at most 128 MiB of HBM per device.

```python
import jax
import jax.numpy as jnp
from jax import lax

MODEL_DIM = 2048
HK = 16
HV = 32
DK = 128
SPAN = 64
TOKENS = 16384
N_HEAD = 8


def draw_write_strength(key, part):
    pick_key, slow_key, fast_key, rough_key = jax.random.split(key, 4)
    slow_share = 0.5
    slow_heads = jax.random.uniform(pick_key, (HV,)) < slow_share
    slow_rate = jax.random.uniform(slow_key, (HV,), minval=0.25, maxval=2.0) * (DK / TOKENS)
    fast_rate = jnp.exp(jax.random.uniform(fast_key, (HV,), minval=jnp.log(0.1), maxval=jnp.log(0.9)))
    base_rate = jnp.where(slow_heads, slow_rate, fast_rate)
    roughness = jax.random.uniform(rough_key, (TOKENS, HV), minval=0.5, maxval=1.5)
    return jnp.minimum(base_rate[None, :] * roughness, 1.0).astype(jnp.bfloat16)


def block_scale(stream_key, extent, shards, smallest, high):
    factor_of = 1.0
    for position, parts in shards:
        steps = jax.random.uniform(jax.random.fold_in(jax.random.fold_in(stream_key, 6), position), (parts,), jnp.float32, smallest / len(shards), high / len(shards))
        factor_of = factor_of * jnp.repeat(jnp.exp(steps), extent[position] // parts).reshape((-1,) + (1,) * (len(extent) - 1 - position))
    return factor_of


def normal_values(own_key, extent, spread, most, cuts=(), held_as=jnp.bfloat16):
    factor_of = block_scale(own_key, extent, cuts, -0.22, 0.18) if cuts else 1.0
    drawn = jax.random.normal(own_key, extent, jnp.float32) * spread * factor_of
    return jnp.minimum(jnp.maximum(drawn, -most), most).astype(held_as)


def setup_inputs(seed: int = 0) -> dict:
    seeds = jax.random.split(jax.random.key(seed), 8)
    return {
        "queries": normal_values(seeds[0], (TOKENS, HK, DK), 1.0, 6.0, ((0, 256),)),
        "key_vectors": normal_values(seeds[1], (TOKENS, HK, DK), 1.0, 6.0, ((0, 256),)),
        "value_vectors": normal_values(seeds[2], (TOKENS, HV, DK), 1.0, 6.0, ((0, 256),)),
        "output_gate": normal_values(seeds[3], (TOKENS, HV, DK), 1.0, 6.0, ((0, 256),)),
        "write_strength": draw_write_strength(jax.random.fold_in(seeds[7], 71), 0),
        "norm_gain": jnp.clip(1.0 + 0.18 * jax.random.normal(seeds[5], (DK,), jnp.float32), 0.099609375, 1.8984375).astype(jnp.bfloat16),
        "output_weight": normal_values(seeds[6], (HV * DK, MODEL_DIM), (HV * DK) ** -0.5, 0.09375, ((0, 8),)),
    }


precise = lax.Precision.HIGHEST
epsilon = 1e-06

def unit_rows(values_in):
    return values_in * lax.rsqrt(lax.optimization_barrier(jnp.sum(values_in * values_in, -1, keepdims=True)) + epsilon)

def span_factors(key_blocks, value_blocks, strength_blocks):
    key_gram = jnp.einsum('...cd,...md->...cm', key_blocks, key_blocks, precision=precise)
    below_diagonal = jnp.tril(key_gram * strength_blocks[..., :, None], -1)
    block_size = key_blocks.shape[-2]
    system = below_diagonal + jnp.eye(block_size, dtype=key_blocks.dtype)
    right_sides = jnp.concatenate([key_blocks * strength_blocks[..., None], value_blocks * strength_blocks[..., None]], -1)
    solved = jax.scipy.linalg.solve_triangular(system, right_sides, lower=True, unit_diagonal=True)
    head_width = key_blocks.shape[-1]
    return (solved[..., :head_width], solved[..., head_width:])

def span_step(carried, pieces):
    query_c, key_c, w_c, u_c = pieces
    scores = jnp.tril(jnp.einsum('...cd,...md->...cm', query_c, key_c, precision=precise))
    corrected = u_c - jnp.einsum('...cd,...de->...ce', w_c, carried, precision=precise)
    outputs = jnp.einsum('...cd,...de->...ce', query_c, carried, precision=precise) + jnp.einsum('...cm,...me->...ce', scores, corrected, precision=precise)
    carried = carried + jnp.einsum('...cd,...ce->...de', key_c, corrected, precision=precise)
    return (carried, outputs)

def reference(queries, key_vectors, value_vectors, output_gate, write_strength, norm_gain, output_weight):
    head_ratio = HV // HK
    query_unit = unit_rows(queries.astype(jnp.float32)) * DK ** (-0.5)
    key_unit = unit_rows(key_vectors.astype(jnp.float32))
    span_count = TOKENS // SPAN

    def one_head(head_index):
        key_index = head_index // head_ratio
        query_rows = lax.dynamic_index_in_dim(query_unit, key_index, 1, False)
        key_rows = lax.dynamic_index_in_dim(key_unit, key_index, 1, False)
        value_rows = lax.dynamic_index_in_dim(value_vectors, head_index, 1, False).astype(jnp.float32)
        strength_rows = lax.dynamic_index_in_dim(write_strength, head_index, 1, False).astype(jnp.float32)
        query_blocks = query_rows.reshape(span_count, SPAN, DK)
        key_blocks = key_rows.reshape(span_count, SPAN, DK)
        value_blocks = value_rows.reshape(span_count, SPAN, DK)
        strength_blocks = strength_rows.reshape(span_count, SPAN)
        w_blocks, u_blocks = span_factors(key_blocks, value_blocks, strength_blocks)
        initial = jnp.zeros((DK, DK), jnp.float32)
        final_state, outputs = lax.scan(span_step, initial, (query_blocks, key_blocks, w_blocks, u_blocks))
        return outputs.reshape(TOKENS, DK)
    core = jnp.transpose(lax.map(one_head, jnp.arange(HV, dtype=jnp.int32)), (1, 0, 2))
    mean_square = lax.optimization_barrier(jnp.mean(core * core, -1, keepdims=True))
    normed = core * lax.rsqrt(mean_square + epsilon) * norm_gain.astype(jnp.float32) * jax.nn.silu(output_gate.astype(jnp.float32))
    gated = normed.astype(jnp.bfloat16).reshape(TOKENS, HV * DK)
    group_rows = HV * DK // N_HEAD
    running = jnp.zeros((TOKENS, MODEL_DIM), jnp.float32)
    for group in range(N_HEAD):
        group_terms = jnp.dot(gated[:, group * group_rows:(group + 1) * group_rows].astype(jnp.float32), output_weight[group * group_rows:(group + 1) * group_rows].astype(jnp.float32), preferred_element_type=jnp.float32)
        running = running + lax.optimization_barrier(group_terms.astype(jnp.bfloat16)).astype(jnp.float32)
    return running.astype(jnp.bfloat16)
```

```python
import functools

import jax
import jax.numpy as jnp
from jax import lax
from jax.experimental import pallas as pl
from jax.experimental.pallas import tpu as pltpu
from jax.sharding import PartitionSpec as P

F32 = jnp.float32
BF16 = jnp.bfloat16
MESH = pl.DeviceIdType.MESH
EPS = 1e-06
C = 128
ROWS = 64
NH = 8
NZ = 8
NX = 4
NY = 4
HV = 4
HK = 2
TOK = ROWS * NH
NB = TOK // C
DM = 2048
HALF = DM // 2
LEVELS = (2, 4, 8, 16, 32, 64)


def nn(a, b):
    return jnp.dot(a, b, preferred_element_type=F32)


def nt(a, b):
    return lax.dot_general(a, b, (((1,), (1,)), ((), ())), preferred_element_type=F32)


def tn(a, b):
    return lax.dot_general(a, b, (((0,), (0,)), ((), ())), preferred_element_type=F32)


def block_rows(c):
    return pl.ds(pl.multiple_of(c * C, C), C)


def kernel(
    q_hbm, k_hbm, v_hbm, g_hbm, b_hbm, gain_ref, w_hbm, out_ref,
    q_in, k_in, v_in, g_in, b_in, w_own, w_sib,
    q_f, k_f, v_f, g_f,
    q_send, k_send, v_send, g_send,
    q_recv, k_recv, v_recv, g_recv,
    masks, rk_row, rk_col, x_u, x_w, wu, chain, before,
    y_q, y_o, gate,
    x_send, x_recv, prefix, x_total, state, s_send, s_in,
    g_mine, g_sib, p_f, p_b, relay_a, relay_b, join_a, join_b,
    minus_a, minus_b, plus_a, plus_b,
    in_sem, own_sem, a2a_send, a2a_recv, w_send_sem, w_recv_sem,
    z_send, z_recv, t_send, t_recv, s_send_sem, s_recv,
    sib_send, sib_recv, rs_send, rs_recv,
):
    seq = lax.axis_index("seq")
    head = lax.axis_index("head")
    x = seq // NZ
    z = lax.rem(seq, NZ)
    y = head // 2
    core = lax.rem(head, 2)
    sibling = y * 2 + (1 - core)

    def on_head(h):
        return (seq, h)

    def on_z(zz):
        return (x * NZ + zz, head)

    def on_x(xx):
        return (xx * NZ + z, head)

    peers = [(2, 0), (2, 1), (1, 0), (1, 1), (3, 0), (3, 1), (0, 1)]

    def head_at(dy, dc):
        return lax.rem(y + dy, NY) * 2 + lax.rem(core + dc, 2)

    barrier = pltpu.get_barrier_semaphore()
    for dy, dc in peers:
        pl.semaphore_signal(barrier, inc=1, device_id=on_head(head_at(dy, dc)), device_id_type=MESH)
    for dz in range(1, NZ):
        pl.semaphore_signal(barrier, inc=1, device_id=on_z(lax.rem(z + dz, NZ)), device_id_type=MESH)
    for dx in range(1, NX):
        pl.semaphore_signal(barrier, inc=1, device_id=on_x(lax.rem(x + dx, NX)), device_id_type=MESH)

    loads = [
        pltpu.make_async_copy(src, dst, in_sem.at[i])
        for i, (src, dst) in enumerate(
            [(k_hbm, k_in), (b_hbm, b_in), (v_hbm, v_in), (q_hbm, q_in), (g_hbm, g_in), (w_hbm, w_own)]
        )
    ]
    for copy in loads:
        copy.start()

    ri = lax.broadcasted_iota(jnp.int32, (C, C), 0)
    ci = lax.broadcasted_iota(jnp.int32, (C, C), 1)
    for i, s in enumerate(LEVELS):
        keep = (ri // (2 * s) == ci // (2 * s)) & (ri // s != ci // s)
        masks[i] = jnp.where(keep, 1.0, 0.0).astype(BF16)

    def to_columns(raw, wide, send, heads):
        per = heads // NH
        wide[...] = raw[...].astype(F32)
        for h in range(heads):
            send[h // per, :, (h % per) * C : (h % per + 1) * C] = wide[
                pl.ds(h, ROWS, stride=heads), :
            ].astype(BF16)

    sends = [(k_send, k_recv), (v_send, v_recv), (q_send, q_recv), (g_send, g_recv)]

    def peer_copy(array, i):
        send, recv = sends[array]
        target = head_at(*peers[i])
        return pltpu.make_async_remote_copy(
            src_ref=send.at[target],
            dst_ref=recv.at[pl.ds(pl.multiple_of(head * ROWS, ROWS), ROWS), :],
            send_sem=a2a_send.at[array, i],
            recv_sem=a2a_recv.at[array, i],
            device_id=on_head(target),
            device_id_type=MESH,
        )

    def own_copy(array):
        send, recv = sends[array]
        return pltpu.make_async_copy(
            send.at[head], recv.at[pl.ds(pl.multiple_of(head * ROWS, ROWS), ROWS), :], own_sem.at[array]
        )

    def start_exchange(array):
        for i in range(len(peers)):
            peer_copy(array, i).start()
        own_copy(array).start()

    def wait_exchange(array):
        own_copy(array).wait()
        for i in range(len(peers)):
            peer_copy(array, i).wait_recv()

    loads[0].wait()
    loads[1].wait()
    to_columns(k_in, k_f, k_send, HK * NH)
    for h in range(NH):
        k_send[h, :, HK * C :] = jnp.zeros((ROWS, C), BF16)
        k_send[h, :, HK * C : HK * C + HV * NH] = b_in[...]
    pl.semaphore_wait(barrier, len(peers) + (NZ - 1) + (NX - 1))
    start_exchange(0)
    loads[2].wait()
    to_columns(v_in, v_f, v_send, HV * NH)
    start_exchange(1)
    loads[3].wait()
    to_columns(q_in, q_f, q_send, HK * NH)
    start_exchange(2)
    loads[4].wait()
    to_columns(g_in, g_f, g_send, HV * NH)
    start_exchange(3)
    weight_copy = pltpu.make_async_remote_copy(
        src_ref=w_hbm, dst_ref=w_sib, send_sem=w_send_sem, recv_sem=w_recv_sem,
        device_id=on_head(sibling), device_id_type=MESH,
    )
    weight_copy.start()

    wait_exchange(0)
    chains = 2

    def invert(step, carry):
        eye = ri == ci
        lower = ri > ci
        todo = []
        for part in range(chains):
            c = step * chains + part
            rows = block_rows(c)
            strengths = k_recv[rows, HK * C :].astype(F32)
            for j in range(HK):
                kb = k_recv[rows, j * C : (j + 1) * C]
                gram = nt(kb, kb)
                diag = jnp.where(eye, gram, 0.0)
                kc = lax.rsqrt(jnp.sum(diag, 1, keepdims=True) + EPS)
                kr = lax.rsqrt(jnp.sum(diag, 0, keepdims=True) + EPS)
                rk_row[j, c] = jnp.broadcast_to(kr, (8, C))
                rk_col[j, c] = jnp.broadcast_to(kc, (C, C))
                scaled = jnp.where(lower, gram * kc * kr, 0.0)
                for n in (2 * j, 2 * j + 1):
                    bc = jnp.sum(jnp.where(ci == head * HV + n, strengths, 0.0), 1, keepdims=True)
                    br = jnp.sum(jnp.where(eye, bc, 0.0), 0, keepdims=True)
                    a = scaled * bc
                    todo.append((n, c, a.astype(BF16), br, kr, jnp.where(eye, 1.0, jnp.where(ri // 2 == ci // 2, -a, 0.0))))
        xs = [t[5] for t in todo]
        for i in range(len(LEVELS)):
            xb = [xx.astype(BF16) for xx in xs]
            right = [nn(t[2] * masks[i], b).astype(BF16) for t, b in zip(todo, xb)]
            xs = [xx - nn(b, r) for xx, b, r in zip(xs, xb, right)]
        for (n, c, _, br, kr, _), xx in zip(todo, xs):
            x_u[n, c] = (xx * br).astype(BF16)
            x_w[n, c] = (xx * (br * kr)).astype(BF16)
        return carry

    lax.fori_loop(0, NB // chains, invert, 0)

    wait_exchange(1)
    chain[...] = jnp.zeros_like(chain)

    def advance(c, carry):
        rows = block_rows(c)
        keys = [k_recv[rows, j * C : (j + 1) * C] for j in range(HK)]
        cols = [rk_col[j, c] for j in range(HK)]
        ws = [nn(x_w[n, c], keys[n // 2]) for n in range(HV)]
        us = [nn(x_u[n, c], v_recv[rows, n * C : (n + 1) * C]) for n in range(HV)]
        scaled = []
        for n in range(HV):
            wu[n, c, :, :C] = ws[n].astype(BF16)
            wu[n, c, :, C:] = us[n].astype(BF16)
            scaled.append(
                jnp.concatenate([ws[n] * -cols[n // 2], us[n] * cols[n // 2]], 1).astype(BF16)
            )
        news = [tn(keys[n // 2], scaled[n]) for n in range(HV)]
        for n in range(HV):
            now = chain[n]
            now_b = now.astype(BF16)
            before[n, c] = now_b
            chain[n] = now + nn(news[n][:, :C].astype(BF16), now_b) + news[n]
        return carry

    lax.fori_loop(0, NB, advance, 0)
    for n in range(HV):
        x_send[n] = chain[n].astype(BF16)

    is_owner = lax.rem(z, 2) == core
    mine = z // 2

    def to_owner(n):
        return pltpu.make_async_remote_copy(
            src_ref=x_send.at[n], dst_ref=x_recv.at[z], send_sem=z_send.at[n], recv_sem=z_recv.at[z],
            device_id=on_z(2 * n + core), device_id_type=MESH,
        )

    def from_z(zz):
        return pltpu.make_async_remote_copy(
            src_ref=x_send.at[0], dst_ref=x_recv.at[zz], send_sem=z_send.at[0], recv_sem=z_recv.at[zz],
            device_id=on_z(zz), device_id_type=MESH,
        )

    for n in range(HV):
        @pl.when(z != 2 * n + core)
        def _():
            to_owner(n).start()

        @pl.when(z == 2 * n + core)
        def _():
            x_recv[z] = x_send[n]

    wait_exchange(2)

    def outputs(c, carry):
        rows = block_rows(c)
        for j in range(HK):
            qb = q_recv[rows, j * C : (j + 1) * C]
            kb = k_recv[rows, j * C : (j + 1) * C]
            qf = qb.astype(F32)
            qc = lax.rsqrt(jnp.sum(qf * qf, 1, keepdims=True) + EPS) * (C ** -0.5)
            scores = jnp.where(ri >= ci, nt(qb, kb) * qc * rk_row[j, c, 0:1, :], 0.0).astype(BF16)
            unit = qf * qc
            for n in (2 * j, 2 * j + 1):
                part = nn(scores, wu[n, c])
                eff = unit - part[:, :C]
                moved = nn(eff.astype(BF16), before[n, c])
                y_q[n, rows, :] = (eff + moved[:, :C]).astype(BF16)
                y_o[n, rows, :] = part[:, C:] + moved[:, C:]
        return carry

    lax.fori_loop(0, NB, outputs, 0)

    def to_x(dx):
        return pltpu.make_async_remote_copy(
            src_ref=prefix.at[NZ], dst_ref=x_total.at[x], send_sem=t_send.at[dx], recv_sem=t_recv.at[x],
            device_id=on_x(x + dx), device_id_type=MESH,
        )

    def from_x(xx):
        return pltpu.make_async_remote_copy(
            src_ref=prefix.at[NZ], dst_ref=x_total.at[xx], send_sem=t_send.at[0], recv_sem=t_recv.at[xx],
            device_id=on_x(xx), device_id_type=MESH,
        )

    def to_z(zz):
        return pltpu.make_async_remote_copy(
            src_ref=s_send.at[zz], dst_ref=s_in.at[mine], send_sem=s_send_sem.at[zz], recv_sem=s_recv.at[mine],
            device_id=on_z(zz), device_id_type=MESH,
        )

    @pl.when(is_owner)
    def _():
        prefix[0] = jnp.zeros((C, 2 * C), BF16)
        total = jnp.zeros((C, 2 * C), F32)
        for zz in range(NZ):
            @pl.when(z != zz)
            def _():
                from_z(zz).wait_recv()

            step = x_recv[zz]
            if zz == 0:
                total = step.astype(F32)
            else:
                total = total + nn(step[:, :C], total.astype(BF16)) + step.astype(F32)
            prefix[zz + 1] = total.astype(BF16)
        for dx in range(1, NX):
            @pl.when(x + dx < NX)
            def _():
                to_x(dx).start()

        state[...] = jnp.zeros_like(state)
        for xx in range(NX - 1):
            @pl.when(xx < x)
            def _():
                from_x(xx).wait_recv()
                step = x_total[xx]
                now = state[...]
                state[...] = now + nn(step[:, :C], now.astype(BF16)) + step[:, C:].astype(F32)

        start = state[...]
        start_b = start.astype(BF16)
        for zz in range(NZ):
            step = prefix[zz]
            here = (start + nn(step[:, :C], start_b) + step[:, C:].astype(F32)).astype(BF16)
            s_send[zz] = here

            @pl.when(z != zz)
            def _():
                to_z(zz).start()

            @pl.when(z == zz)
            def _():
                s_in[mine] = s_send[zz]

    wait_exchange(3)
    gain = gain_ref[...].astype(F32)

    def gates(c, carry):
        rows = block_rows(c)
        for n in range(HV):
            v = g_recv[rows, n * C : (n + 1) * C].astype(F32)
            gate[rows, n * C : (n + 1) * C] = v / (1.0 + jnp.exp(-v)) * gain
        return carry

    lax.fori_loop(0, NB, gates, 0)

    def to_sibling(n):
        cols = slice(n * C, (n + 1) * C)
        return pltpu.make_async_remote_copy(
            src_ref=g_mine.at[1 - core, :, cols], dst_ref=g_sib.at[:, cols],
            send_sem=sib_send.at[n], recv_sem=sib_recv.at[n],
            device_id=on_head(sibling), device_id_type=MESH,
        )

    for n in range(HV):
        @pl.when(z != 2 * n + core)
        def _():
            pltpu.make_async_remote_copy(
                src_ref=s_send.at[0], dst_ref=s_in.at[n], send_sem=s_send_sem.at[0], recv_sem=s_recv.at[n],
                device_id=on_z(2 * n + core), device_id_type=MESH,
            ).wait_recv()

        now = s_in[n]
        for c in range(NB):
            rows = slice(c * C, (c + 1) * C)
            values = nn(y_q[n, rows, :], now) + y_o[n, rows, :]
            spread = lax.rsqrt(jnp.mean(values * values, -1, keepdims=True) + EPS)
            gated = (values * spread * gate[rows, n * C : (n + 1) * C]).astype(BF16)
            for side in range(2):
                g_mine[side, c * ROWS : (c + 1) * ROWS, n * C : (n + 1) * C] = gated[
                    side * ROWS : (side + 1) * ROWS
                ]
        to_sibling(n).start()

    loads[5].wait()
    weight_copy.wait_recv()
    for n in range(HV):
        to_sibling(n).wait_recv()

    tile = 256

    def project(first):
        def one(t, carry):
            cols = pl.ds(pl.multiple_of(first + t * tile, tile), tile)
            value = nn(g_mine[core], w_own[:, cols]) + nn(g_sib[...], w_sib[:, cols])
            p_f[:, cols] = value
            p_b[:, cols] = value.astype(BF16)
            return carry

        lax.fori_loop(0, HALF // tile, one, 0)

    def rows_of(dy):
        return pl.ds(pl.multiple_of(lax.rem(y + dy, NY) * ROWS, ROWS), ROWS)

    a_cols, b_cols = slice(0, HALF), slice(HALF, DM)

    def ring(i, src, dst, dy):
        return pltpu.make_async_remote_copy(
            src_ref=src, dst_ref=dst, send_sem=rs_send.at[i], recv_sem=rs_recv.at[i],
            device_id=on_head(lax.rem(y + dy, NY) * 2 + core), device_id_type=MESH,
        )

    copies = [
        ring(0, p_b.at[rows_of(2), a_cols], relay_a, 1),
        ring(1, p_b.at[rows_of(3), a_cols], plus_a, 3),
        ring(2, p_b.at[rows_of(2), b_cols], relay_b, 3),
        ring(3, p_b.at[rows_of(1), b_cols], minus_b, 1),
        ring(4, join_a, minus_a, 1),
        ring(5, join_b, plus_b, 3),
    ]
    project(0)
    copies[0].start()
    copies[1].start()
    project(HALF)
    copies[2].start()
    copies[3].start()
    copies[0].wait_recv()
    join_a[...] = (p_f[rows_of(1), a_cols] + relay_a[...].astype(F32)).astype(BF16)
    copies[4].start()
    copies[2].wait_recv()
    join_b[...] = (p_f[rows_of(3), b_cols] + relay_b[...].astype(F32)).astype(BF16)
    copies[5].start()
    copies[1].wait_recv()
    copies[3].wait_recv()
    copies[4].wait_recv()
    out_ref[:, a_cols] = (
        p_f[rows_of(0), a_cols] + minus_a[...].astype(F32) + plus_a[...].astype(F32)
    ).astype(BF16)
    copies[5].wait_recv()
    out_ref[:, b_cols] = (
        p_f[rows_of(0), b_cols] + minus_b[...].astype(F32) + plus_b[...].astype(F32)
    ).astype(BF16)

    for array in range(4):
        for i in range(len(peers)):
            peer_copy(array, i).wait_send()
    weight_copy.wait_send()
    for n in range(HV):
        to_sibling(n).wait_send()

        @pl.when(z != 2 * n + core)
        def _():
            to_owner(n).wait_send()

    @pl.when(is_owner)
    def _():
        for dx in range(1, NX):
            @pl.when(x + dx < NX)
            def _():
                to_x(dx).wait_send()

        for zz in range(NZ):
            @pl.when(z != zz)
            def _():
                to_z(zz).wait_send()

    for copy in copies:
        copy.wait_send()


def per_device(queries, key_vectors, value_vectors, output_gate, write_strength, norm_gain, output_weight):
    any_space = pl.BlockSpec(memory_space=pl.ANY)
    vmem = pl.BlockSpec(memory_space=pltpu.VMEM)
    dma = pltpu.SemaphoreType.DMA
    v = pltpu.VMEM
    kh, vh = HK * NH, HV * NH
    scratch = [
        v((ROWS * kh, C), BF16), v((ROWS * kh, C), BF16), v((ROWS * vh, C), BF16), v((ROWS * vh, C), BF16),
        v((ROWS, vh), BF16), v((HV * C, DM), BF16), v((HV * C, DM), BF16),
        v((ROWS * kh, C), F32), v((ROWS * kh, C), F32), v((ROWS * vh, C), F32), v((ROWS * vh, C), F32),
        v((NH, ROWS, HK * C), BF16), v((NH, ROWS, HK * C + C), BF16), v((NH, ROWS, HV * C), BF16), v((NH, ROWS, HV * C), BF16),
        v((TOK, HK * C), BF16), v((TOK, HK * C + C), BF16), v((TOK, HV * C), BF16), v((TOK, HV * C), BF16),
        v((len(LEVELS), C, C), BF16), v((HK, NB, 8, C), F32), v((HK, NB, C, C), F32),
        v((HV, NB, C, C), BF16), v((HV, NB, C, C), BF16), v((HV, NB, C, 2 * C), BF16),
        v((HV, C, 2 * C), F32), v((HV, NB, C, 2 * C), BF16),
        v((HV, TOK, C), BF16), v((HV, TOK, C), F32), v((TOK, HV * C), F32),
        v((HV, C, 2 * C), BF16), v((NZ, C, 2 * C), BF16), v((NZ + 1, C, 2 * C), BF16), v((NX, C, 2 * C), BF16),
        v((C, C), F32), v((NZ, C, C), BF16), v((HV, C, C), BF16),
        v((2, NY * ROWS, HV * C), BF16), v((NY * ROWS, HV * C), BF16),
        v((NY * ROWS, DM), F32), v((NY * ROWS, DM), BF16),
        v((ROWS, HALF), BF16), v((ROWS, HALF), BF16), v((ROWS, HALF), BF16), v((ROWS, HALF), BF16),
        v((ROWS, HALF), BF16), v((ROWS, HALF), BF16), v((ROWS, HALF), BF16), v((ROWS, HALF), BF16),
        dma((6,)), dma((4,)), dma((4, 7)), dma((4, 7)), dma, dma,
        dma((HV,)), dma((NZ,)), dma((NX,)), dma((NX,)), dma((NZ,)), dma((HV,)),
        dma((HV,)), dma((HV,)), dma((6,)), dma((6,)),
    ]
    return pl.pallas_call(
        kernel,
        out_shape=jax.ShapeDtypeStruct((ROWS, DM), BF16),
        in_specs=[any_space] * 5 + [vmem, any_space],
        out_specs=vmem,
        scratch_shapes=scratch,
        compiler_params=pltpu.CompilerParams(
            collective_id=0, has_side_effects=True, vmem_limit_bytes=52 * 1024 * 1024
        ),
    )(
        queries.reshape(ROWS * kh, C),
        key_vectors.reshape(ROWS * kh, C),
        value_vectors.reshape(ROWS * vh, C),
        output_gate.reshape(ROWS * vh, C),
        write_strength,
        norm_gain.reshape(1, C),
        output_weight,
    )


def solution(mesh):
    placed = (
        P(("seq", "head"), None, None),
        P(("seq", "head"), None, None),
        P(("seq", "head"), None, None),
        P(("seq", "head"), None, None),
        P(("seq", "head"), None),
        P(),
        P("head", None),
    )
    return jax.shard_map(
        per_device, mesh=mesh, in_specs=placed, out_specs=P(("seq", "head"), None), check_vma=False
    )
```

```python
import functools

import jax
import jax.numpy as jnp
from jax import lax
from jax.experimental import pallas as pl
from jax.experimental.pallas import tpu as pltpu
from jax.sharding import PartitionSpec as P

F32 = jnp.float32
BF16 = jnp.bfloat16
MESH = pl.DeviceIdType.MESH
EPS = 1e-06
C = 128
ROWS = 64
NH = 8
NZ = 8
NX = 4
NY = 4
HV = 4
HK = 2
TOK = ROWS * NH
NB = TOK // C
DM = 2048
HALF = DM // 2
LEVELS = (2, 4, 8, 16, 32, 64)
KROWS = ROWS + 16


def nn(a, b):
    return jnp.dot(a, b, preferred_element_type=F32)


def nt(a, b):
    return lax.dot_general(a, b, (((1,), (1,)), ((), ())), preferred_element_type=F32)


def tn(a, b):
    return lax.dot_general(a, b, (((0,), (0,)), ((), ())), preferred_element_type=F32)


def block_rows(c):
    return pl.ds(pl.multiple_of(c * C, C), C)


def lower_rows(m, s):
    return jnp.concatenate([m[a + s : a + 2 * s] for a in range(0, C, 2 * s)], 0)


def double(xs, offs, s):
    bs = [x.astype(BF16) for x in xs]
    if s < 16:
        rights = [nn(o, b).astype(BF16) for o, b in zip(offs, bs)]
        return [x - nn(b, r) for x, b, r in zip(xs, bs, rights)]
    rights = [nn(lower_rows(o, s), b).astype(BF16) for o, b in zip(offs, bs)]
    zero = jnp.zeros((s, C), BF16)
    count = C // (2 * s)
    fulls = [
        jnp.concatenate(sum([[zero, r[i * s : (i + 1) * s]] for i in range(count)], []), 0) for r in rights
    ]
    steps = [nn(lower_rows(b, s), f) for b, f in zip(bs, fulls)]
    return [
        jnp.concatenate(
            sum(
                [
                    [x[2 * i * s : (2 * i + 1) * s], x[(2 * i + 1) * s : (2 * i + 2) * s] - d[i * s : (i + 1) * s]]
                    for i in range(count)
                ],
                [],
            ),
            0,
        )
        for x, d in zip(xs, steps)
    ]


def kernel(
    q_hbm, k_hbm, v_hbm, g_hbm, b_hbm, gain_ref, w_hbm, out_ref,
    q_in, k_in, v_in, g_in, b_in, w_own, w_sib,
    q_f, k_f, v_f, g_f, b_f,
    q_send, k_send, v_send, g_send,
    q_recv, k_recv, v_recv, g_recv,
    masks, rk_row, rk_col, x_u, moves, wu, ku, before,
    y_q, y_o, gate,
    t_mine, l_mine, t_all, l_all, t_join, t_pre, l_pre, t_row, l_row, state, s_send, s_in,
    g_mine, g_sib, p_f, p_b, relay_a, relay_b, join_a, join_b,
    minus_a, minus_b, plus_a, plus_b,
    in_sem, own_sem, a2a_send, a2a_recv, w_send_sem, w_recv_sem,
    t_send, t_recv, l_send, l_recv, tr_send, tr_recv, lr_send, lr_recv, s_send_sem, s_recv,
    sib_send, sib_recv, rs_send, rs_recv,
):
    seq = lax.axis_index("seq")
    head = lax.axis_index("head")
    x = seq // NZ
    z = lax.rem(seq, NZ)
    y = head // 2
    core = lax.rem(head, 2)
    sibling = y * 2 + (1 - core)

    def on_head(h):
        return (seq, h)

    def on_z(zz):
        return (x * NZ + zz, head)

    def on_x(xx):
        return (xx * NZ + z, head)

    peers = [(0, 1), (3, 0), (3, 1), (1, 0), (1, 1), (2, 0), (2, 1)]

    def head_at(dy, dc):
        return lax.rem(y + dy, NY) * 2 + lax.rem(core + dc, 2)

    barrier = pltpu.get_barrier_semaphore()
    for dy, dc in peers:
        pl.semaphore_signal(barrier, inc=1, device_id=on_head(head_at(dy, dc)), device_id_type=MESH)
    for dz in range(1, NZ):
        pl.semaphore_signal(barrier, inc=1, device_id=on_z(lax.rem(z + dz, NZ)), device_id_type=MESH)
    for dx in range(1, NX):
        pl.semaphore_signal(barrier, inc=1, device_id=on_x(lax.rem(x + dx, NX)), device_id_type=MESH)

    loads = [
        pltpu.make_async_copy(src, dst, in_sem.at[i])
        for i, (src, dst) in enumerate(
            [(k_hbm, k_in), (b_hbm, b_in), (v_hbm, v_in), (q_hbm, q_in), (g_hbm, g_in), (w_hbm, w_own)]
        )
    ]
    for copy in loads:
        copy.start()

    ri = lax.broadcasted_iota(jnp.int32, (C, C), 0)
    ci = lax.broadcasted_iota(jnp.int32, (C, C), 1)
    for i, s in enumerate(LEVELS):
        keep = (ri // (2 * s) == ci // (2 * s)) & (ri // s != ci // s)
        masks[i] = jnp.where(keep, 1.0, 0.0).astype(BF16)

    def to_columns(raw, wide, send, heads):
        per = heads // NH
        wide[...] = raw[...].astype(F32)
        for h in range(heads):
            send[h // per, :ROWS, (h % per) * C : (h % per + 1) * C] = wide[
                pl.ds(h, ROWS, stride=heads), :
            ].astype(BF16)

    sends = [(k_send, k_recv), (v_send, v_recv), (q_send, q_recv), (g_send, g_recv)]

    def peer_copy(array, i):
        send, recv = sends[array]
        target = head_at(*peers[i])
        return pltpu.make_async_remote_copy(
            src_ref=send.at[target],
            dst_ref=recv.at[head],
            send_sem=a2a_send.at[array, i],
            recv_sem=a2a_recv.at[array, i],
            device_id=on_head(target),
            device_id_type=MESH,
        )

    def own_copy(array):
        send, recv = sends[array]
        return pltpu.make_async_copy(send.at[head], recv.at[head], own_sem.at[array])

    def start_exchange(array):
        for i in range(len(peers)):
            peer_copy(array, i).start()
        own_copy(array).start()

    def wait_exchange(array):
        own_copy(array).wait()
        for i in range(len(peers)):
            peer_copy(array, i).wait_recv()

    def block(recv, c, cols):
        return jnp.concatenate([recv[2 * c + i, :ROWS, cols] for i in range(2)], 0)

    loads[0].wait()
    loads[1].wait()
    to_columns(k_in, k_f, k_send, HK * NH)
    lanes = lax.broadcasted_iota(jnp.int32, (ROWS, C), 1) - ROWS * lax.rem(head, 2)
    place = jnp.where(lanes == lax.broadcasted_iota(jnp.int32, (ROWS, C), 0), 1.0, 0.0).astype(BF16)
    b_f[: HV * NH, :] = nn(b_in[...], place)
    b_f[HV * NH :, :] = jnp.zeros((16, C), F32)
    for h in range(NH):
        k_send[h, ROWS:, :C] = b_f[h * HV : h * HV + 16, :].astype(BF16)
        k_send[h, ROWS:, C:] = jnp.zeros((16, C), BF16)
    pl.semaphore_wait(barrier, len(peers) + (NZ - 1) + (NX - 1))
    start_exchange(0)
    loads[2].wait()
    to_columns(v_in, v_f, v_send, HV * NH)
    start_exchange(1)
    loads[3].wait()
    to_columns(q_in, q_f, q_send, HK * NH)
    start_exchange(2)
    loads[4].wait()
    to_columns(g_in, g_f, g_send, HV * NH)
    start_exchange(3)
    weight_copy = pltpu.make_async_remote_copy(
        src_ref=w_hbm, dst_ref=w_sib, send_sem=w_send_sem, recv_sem=w_recv_sem,
        device_id=on_head(sibling), device_id_type=MESH,
    )
    weight_copy.start()

    eye = ri == ci

    def invert(blocks):
        todo = []
        for c in blocks:
            sums = sum(k_recv[2 * c + i, ROWS:, :C].astype(F32) for i in range(2))
            for j in range(HK):
                kb = block(k_recv, c, slice(j * C, (j + 1) * C))
                gram = nt(kb, kb)
                diag = jnp.where(eye, gram, 0.0)
                kc = lax.rsqrt(jnp.sum(diag, 1, keepdims=True) + EPS)
                kr = lax.rsqrt(jnp.sum(diag, 0, keepdims=True) + EPS)
                rk_row[j, c] = jnp.broadcast_to(kr, (8, C))
                rk_col[j, c] = jnp.broadcast_to(kc, (C, C))
                scaled = jnp.where(ri > ci, gram * kc * kr, 0.0)
                for n in (2 * j, 2 * j + 1):
                    br = sums[n : n + 1]
                    bc = jnp.sum(jnp.where(eye, br, 0.0), 1, keepdims=True)
                    a = scaled * bc
                    first = jnp.where(eye, 1.0, jnp.where(ri // 2 == ci // 2, -a, 0.0))
                    todo.append((n, c, a.astype(BF16), br, kr, kc, kb, first))
        xs = [t[-1] for t in todo]
        for i, s in enumerate(LEVELS):
            xs = double(xs, [t[2] * masks[i] for t in todo], s)
        ws = []
        for (n, c, _, br, kr, kc, kb, _), x in zip(todo, xs):
            right = x * br
            x_u[n, c] = right.astype(BF16)
            ws.append(nn((right * kr).astype(BF16), kb))
        for (n, c, _, br, kr, kc, kb, _), w in zip(todo, ws):
            wu[n, c, :, :C] = w.astype(BF16)
            moves[n, c] = tn(kb, (w * -kc).astype(BF16))

    def wait_keys(some):
        for i in some:
            peer_copy(0, i).wait_recv()

    own_copy(0).wait()
    wait_keys((0, 1, 2))
    invert((y, lax.rem(y + 1, NY)))
    wait_keys((3, 4, 5, 6))
    invert((lax.rem(y + 3, NY), lax.rem(y + 2, NY)))

    is_owner = lax.rem(z, 2) == core
    mine = z // 2

    def to_owner(mine_ref, all_ref, send, recv, n):
        return pltpu.make_async_remote_copy(
            src_ref=mine_ref.at[n], dst_ref=all_ref.at[z], send_sem=send.at[n], recv_sem=recv.at[z],
            device_id=on_z(2 * n + core), device_id_type=MESH,
        )

    def from_z(mine_ref, all_ref, send, recv, zz):
        return pltpu.make_async_remote_copy(
            src_ref=mine_ref.at[0], dst_ref=all_ref.at[zz], send_sem=send.at[0], recv_sem=recv.at[zz],
            device_id=on_z(zz), device_id_type=MESH,
        )

    t_refs = (t_mine, t_all, t_send, t_recv)
    l_refs = (l_mine, l_all, l_send, l_recv)

    def hand_in(refs):
        for n in range(HV):
            @pl.when(z != 2 * n + core)
            def _():
                to_owner(*refs, n).start()

            @pl.when(z == 2 * n + core)
            def _():
                refs[1][z] = refs[0][n]

    def gather(refs):
        for zz in range(NZ):
            @pl.when(z != zz)
            def _():
                from_z(*refs, zz).wait_recv()

    ts = [moves[n, 0] for n in range(HV)]
    for n in range(HV):
        before[n, 0] = jnp.zeros((C, 2 * C), BF16)
    for c in range(1, NB):
        tb = [t.astype(BF16) for t in ts]
        for n in range(HV):
            before[n, c, :, :C] = tb[n]
        step = [moves[n, c] for n in range(HV)]
        ts = [t + nn(m.astype(BF16), b) + m for t, m, b in zip(ts, step, tb)]
    for n in range(HV):
        t_mine[n] = ts[n].astype(BF16)
    hand_in(t_refs)

    wait_exchange(1)
    pair = 2

    def values(step, carry):
        todo = [(n, step * pair + i) for i in range(pair) for n in range(HV)]
        us = [nn(x_u[n, c], block(v_recv, c, slice(n * C, (n + 1) * C))) for n, c in todo]
        for (n, c), u in zip(todo, us):
            wu[n, c, :, C:] = u.astype(BF16)
        for (n, c), u in zip(todo, us):
            j = n // 2
            kb = block(k_recv, c, slice(j * C, (j + 1) * C))
            ku[n, c] = tn(kb, (u * rk_col[j, c]).astype(BF16))
        return carry

    lax.fori_loop(0, NB // pair, values, 0)
    ls = [ku[n, 0] for n in range(HV)]
    for c in range(1, NB):
        lb = [l.astype(BF16) for l in ls]
        for n in range(HV):
            before[n, c, :, C:] = lb[n]
        ls = [ls[n] + nn(moves[n, c].astype(BF16), lb[n]) + ku[n, c] for n in range(HV)]
    for n in range(HV):
        l_mine[n] = ls[n].astype(BF16)
    hand_in(l_refs)

    wait_exchange(2)

    def outputs(c, carry):
        rows = block_rows(c)
        for j in range(HK):
            qb = block(q_recv, c, slice(j * C, (j + 1) * C))
            kb = block(k_recv, c, slice(j * C, (j + 1) * C))
            qf = qb.astype(F32)
            qc = lax.rsqrt(jnp.sum(qf * qf, 1, keepdims=True) + EPS) * (C ** -0.5)
            scores = jnp.where(ri >= ci, nt(qb, kb) * qc * rk_row[j, c, 0:1, :], 0.0).astype(BF16)
            unit = qf * qc
            for n in (2 * j, 2 * j + 1):
                part = nn(scores, wu[n, c])
                eff = unit - part[:, :C]
                moved = nn(eff.astype(BF16), before[n, c])
                y_q[n, rows, :] = (eff + moved[:, :C]).astype(BF16)
                y_o[n, rows, :] = part[:, C:] + moved[:, C:]
        return carry

    lax.fori_loop(0, NB, outputs, 0)

    wait_exchange(3)
    gain = gain_ref[...].astype(F32)

    def gates(c, carry):
        rows = block_rows(c)
        for n in range(HV):
            v = block(g_recv, c, slice(n * C, (n + 1) * C)).astype(F32)
            gate[rows, n * C : (n + 1) * C] = v / (1.0 + jnp.exp(-v)) * gain
        return carry

    lax.fori_loop(0, NB, gates, 0)

    tree = [
        [((1,), 0), ((3,), 2), ((5,), 4), ((7,), 6)],
        [((2, 3), 1), ((6, 7), 5)],
        [((4, 5, 6, 7), 3)],
    ]

    def to_x(row, send, recv, dx):
        return pltpu.make_async_remote_copy(
            src_ref=row.at[x], dst_ref=row.at[x], send_sem=send.at[dx], recv_sem=recv.at[x],
            device_id=on_x(x + dx), device_id_type=MESH,
        )

    def from_x(row, send, recv, xx):
        return pltpu.make_async_remote_copy(
            src_ref=row.at[xx], dst_ref=row.at[xx], send_sem=send.at[0], recv_sem=recv.at[xx],
            device_id=on_x(xx), device_id_type=MESH,
        )

    t_line = (t_row, tr_send, tr_recv)
    l_line = (l_row, lr_send, lr_recv)

    def to_z(zz):
        return pltpu.make_async_remote_copy(
            src_ref=s_send.at[zz], dst_ref=s_in.at[mine], send_sem=s_send_sem.at[zz], recv_sem=s_recv.at[mine],
            device_id=on_z(zz), device_id_type=MESH,
        )

    @pl.when(is_owner)
    def _():
        gather(t_refs)
        now = [t_all[zz] for zz in range(NZ)]
        for i, level in enumerate(tree):
            news = {}
            m = 0
            for laters, earlier in level:
                left = jnp.concatenate([now[later] for later in laters], 0)
                t_join[i, m * C : (m + len(laters)) * C] = left
                moved = nn(left, now[earlier])
                for a, later in enumerate(laters):
                    both = now[later].astype(F32) + now[earlier].astype(F32)
                    news[later] = (both + moved[a * C : (a + 1) * C]).astype(BF16)
                m += len(laters)
            for later in news:
                now[later] = news[later]
        for zz in range(NZ):
            t_pre[zz] = now[zz]
        t_row[x] = now[NZ - 1]
        for dx in range(1, NX):
            @pl.when((x > 0) & (x + dx < NX))
            def _():
                to_x(*t_line, dx).start()

        gather(l_refs)
        for zz in range(NZ):
            l_pre[zz] = l_all[zz].astype(F32)
        for i, level in enumerate(tree):
            m = 0
            for laters, earlier in level:
                first = l_pre[earlier]
                moved = nn(t_join[i, m * C : (m + len(laters)) * C], first.astype(BF16))
                for a, later in enumerate(laters):
                    l_pre[later] = l_pre[later] + first + moved[a * C : (a + 1) * C]
                m += len(laters)
        l_row[x] = l_pre[NZ - 1].astype(BF16)
        for dx in range(1, NX):
            @pl.when(x + dx < NX)
            def _():
                to_x(*l_line, dx).start()

        state[...] = jnp.zeros_like(state)
        for xx in range(NX - 1):
            @pl.when(xx < x)
            def _():
                from_x(*l_line, xx).wait_recv()
                row = l_row[xx].astype(F32)
                if xx == 0:
                    state[...] = row
                else:
                    from_x(*t_line, xx).wait_recv()
                    held = state[...]
                    state[...] = held + nn(t_row[xx], held.astype(BF16)) + row

        start = state[...]
        start_b = start.astype(BF16)
        for zz in range(NZ):
            if zz == 0:
                s_send[zz] = start_b
            else:
                s_send[zz] = (start + nn(t_pre[zz - 1], start_b) + l_pre[zz - 1]).astype(BF16)

            @pl.when(z != zz)
            def _():
                to_z(zz).start()

            @pl.when(z == zz)
            def _():
                s_in[mine] = s_send[zz]

    def to_sibling(n):
        cols = slice(n * C, (n + 1) * C)
        return pltpu.make_async_remote_copy(
            src_ref=g_mine.at[1 - core, :, cols], dst_ref=g_sib.at[:, cols],
            send_sem=sib_send.at[n], recv_sem=sib_recv.at[n],
            device_id=on_head(sibling), device_id_type=MESH,
        )

    for n in range(HV):
        @pl.when(z != 2 * n + core)
        def _():
            pltpu.make_async_remote_copy(
                src_ref=s_send.at[0], dst_ref=s_in.at[n], send_sem=s_send_sem.at[0], recv_sem=s_recv.at[n],
                device_id=on_z(2 * n + core), device_id_type=MESH,
            ).wait_recv()

        now = s_in[n]
        for c in range(NB):
            rows = slice(c * C, (c + 1) * C)
            values = nn(y_q[n, rows, :], now) + y_o[n, rows, :]
            spread = lax.rsqrt(jnp.mean(values * values, -1, keepdims=True) + EPS)
            gated = (values * spread * gate[rows, n * C : (n + 1) * C]).astype(BF16)
            for side in range(2):
                g_mine[side, c * ROWS : (c + 1) * ROWS, n * C : (n + 1) * C] = gated[
                    side * ROWS : (side + 1) * ROWS
                ]
        to_sibling(n).start()

    loads[5].wait()
    weight_copy.wait_recv()
    for n in range(HV):
        to_sibling(n).wait_recv()

    tile, piece = 256, 512

    def project(first):
        def one(t, carry):
            cols = pl.ds(pl.multiple_of(first + t * tile, tile), tile)
            value = nn(g_mine[core], w_own[:, cols]) + nn(g_sib[...], w_sib[:, cols])
            p_f[:, cols] = value
            p_b[:, cols] = value.astype(BF16)
            return carry

        lax.fori_loop(0, piece // tile, one, 0)

    def rows_of(dy):
        return pl.ds(pl.multiple_of(lax.rem(y + dy, NY) * ROWS, ROWS), ROWS)

    def ring(i, src, dst, dy):
        return pltpu.make_async_remote_copy(
            src_ref=src, dst_ref=dst, send_sem=rs_send.at[i], recv_sem=rs_recv.at[i],
            device_id=on_head(lax.rem(y + dy, NY) * 2 + core), device_id_type=MESH,
        )

    a_cols, b_cols = slice(0, HALF), slice(HALF, DM)
    near = [slice(0, piece), slice(piece, HALF)]
    far = [slice(HALF, HALF + piece), slice(HALF + piece, DM)]
    relays_a = [ring(i, p_b.at[rows_of(2), near[i]], relay_a.at[:, near[i]], 1) for i in range(2)]
    relays_b = [ring(2 + i, p_b.at[rows_of(2), far[i]], relay_b.at[:, near[i]], 3) for i in range(2)]
    alone_a = ring(4, p_b.at[rows_of(3), a_cols], plus_a, 3)
    alone_b = ring(5, p_b.at[rows_of(1), b_cols], minus_b, 1)
    joins_a = [ring(6 + i, join_a.at[:, near[i]], minus_a.at[:, near[i]], 1) for i in range(2)]
    joins_b = [ring(8 + i, join_b.at[:, near[i]], plus_b.at[:, near[i]], 3) for i in range(2)]
    copies = relays_a + relays_b + [alone_a, alone_b] + joins_a + joins_b
    for i in range(2):
        project(i * piece)
        relays_a[i].start()
        project(HALF + i * piece)
        relays_b[i].start()
    alone_a.start()
    alone_b.start()
    for i in range(2):
        relays_a[i].wait_recv()
        join_a[:, near[i]] = (p_f[rows_of(1), near[i]] + relay_a[:, near[i]].astype(F32)).astype(BF16)
        joins_a[i].start()
        relays_b[i].wait_recv()
        join_b[:, near[i]] = (p_f[rows_of(3), far[i]] + relay_b[:, near[i]].astype(F32)).astype(BF16)
        joins_b[i].start()
    alone_a.wait_recv()
    alone_b.wait_recv()
    for i in range(2):
        joins_a[i].wait_recv()
        out_ref[:, near[i]] = (
            p_f[rows_of(0), near[i]] + minus_a[:, near[i]].astype(F32) + plus_a[:, near[i]].astype(F32)
        ).astype(BF16)
        joins_b[i].wait_recv()
        out_ref[:, far[i]] = (
            p_f[rows_of(0), far[i]] + minus_b[:, near[i]].astype(F32) + plus_b[:, near[i]].astype(F32)
        ).astype(BF16)

    for array in range(4):
        for i in range(len(peers)):
            peer_copy(array, i).wait_send()
    weight_copy.wait_send()
    for n in range(HV):
        to_sibling(n).wait_send()

        @pl.when(z != 2 * n + core)
        def _():
            to_owner(*t_refs, n).wait_send()
            to_owner(*l_refs, n).wait_send()

    @pl.when(is_owner)
    def _():
        for dx in range(1, NX):
            @pl.when((x > 0) & (x + dx < NX))
            def _():
                to_x(*t_line, dx).wait_send()

            @pl.when(x + dx < NX)
            def _():
                to_x(*l_line, dx).wait_send()

        for zz in range(NZ):
            @pl.when(z != zz)
            def _():
                to_z(zz).wait_send()

    for copy in copies:
        copy.wait_send()


def per_device(queries, key_vectors, value_vectors, output_gate, write_strength, norm_gain, output_weight):
    any_space = pl.BlockSpec(memory_space=pl.ANY)
    vmem = pl.BlockSpec(memory_space=pltpu.VMEM)
    dma = pltpu.SemaphoreType.DMA
    v = pltpu.VMEM
    kh, vh = HK * NH, HV * NH
    half = v((ROWS, HALF), BF16)
    scratch = [
        v((ROWS * kh, C), BF16), v((ROWS * kh, C), BF16), v((ROWS * vh, C), BF16), v((ROWS * vh, C), BF16),
        v((vh, ROWS), BF16), v((HV * C, DM), BF16), v((HV * C, DM), BF16),
        v((ROWS * kh, C), F32), v((ROWS * kh, C), F32), v((ROWS * vh, C), F32), v((ROWS * vh, C), F32), v((vh + 16, C), F32),
        v((NH, ROWS, HK * C), BF16), v((NH, KROWS, HK * C), BF16), v((NH, ROWS, HV * C), BF16), v((NH, ROWS, HV * C), BF16),
        v((NH, ROWS, HK * C), BF16), v((NH, KROWS, HK * C), BF16), v((NH, ROWS, HV * C), BF16), v((NH, ROWS, HV * C), BF16),
        v((len(LEVELS), C, C), BF16), v((HK, NB, 8, C), F32), v((HK, NB, C, C), F32),
        v((HV, NB, C, C), BF16), v((HV, NB, C, C), F32), v((HV, NB, C, 2 * C), BF16), v((HV, NB, C, C), F32),
        v((HV, NB, C, 2 * C), BF16),
        v((HV, TOK, C), BF16), v((HV, TOK, C), F32), v((TOK, HV * C), F32),
        v((HV, C, C), BF16), v((HV, C, C), BF16), v((NZ, C, C), BF16), v((NZ, C, C), BF16),
        v((3, 4 * C, C), BF16), v((NZ, C, C), BF16), v((NZ, C, C), F32), v((NX, C, C), BF16), v((NX, C, C), BF16),
        v((C, C), F32), v((NZ, C, C), BF16), v((HV, C, C), BF16),
        v((2, NY * ROWS, HV * C), BF16), v((NY * ROWS, HV * C), BF16),
        v((NY * ROWS, DM), F32), v((NY * ROWS, DM), BF16),
        half, half, half, half, half, half, half, half,
        dma((6,)), dma((4,)), dma((4, 7)), dma((4, 7)), dma, dma,
        dma((HV,)), dma((NZ,)), dma((HV,)), dma((NZ,)), dma((NX,)), dma((NX,)), dma((NX,)), dma((NX,)),
        dma((NZ,)), dma((HV,)),
        dma((HV,)), dma((HV,)), dma((10,)), dma((10,)),
    ]
    return pl.pallas_call(
        kernel,
        out_shape=jax.ShapeDtypeStruct((ROWS, DM), BF16),
        in_specs=[any_space] * 5 + [vmem, any_space],
        out_specs=vmem,
        scratch_shapes=scratch,
        compiler_params=pltpu.CompilerParams(
            collective_id=0, has_side_effects=True, vmem_limit_bytes=60 * 1024 * 1024
        ),
    )(
        queries.reshape(ROWS * kh, C),
        key_vectors.reshape(ROWS * kh, C),
        value_vectors.reshape(ROWS * vh, C),
        output_gate.reshape(ROWS * vh, C),
        write_strength.T,
        norm_gain.reshape(1, C),
        output_weight,
    )


def solution(mesh):
    placed = (
        P(("seq", "head"), None, None),
        P(("seq", "head"), None, None),
        P(("seq", "head"), None, None),
        P(("seq", "head"), None, None),
        P(("seq", "head"), None),
        P(),
        P("head", None),
    )
    return jax.shard_map(
        per_device, mesh=mesh, in_specs=placed, out_specs=P(("seq", "head"), None), check_vma=False
    )
```

```python
import functools

import jax
import jax.numpy as jnp
from jax import lax
from jax.experimental import pallas as pl
from jax.experimental.pallas import tpu as pltpu
from jax.sharding import PartitionSpec as P

F32 = jnp.float32
BF16 = jnp.bfloat16
MESH = pl.DeviceIdType.MESH
EPS = 1e-06
C = 128
ROWS = 64
NH = 8
NZ = 8
NX = 4
NY = 4
HV = 4
HK = 2
TOK = ROWS * NH
NB = TOK // C
DM = 2048
HALF = DM // 2
LEVELS = (2, 4, 8, 16, 32, 64)
KROWS = ROWS + 16


def nn(a, b):
    return jnp.dot(a, b, preferred_element_type=F32)


def nt(a, b):
    return lax.dot_general(a, b, (((1,), (1,)), ((), ())), preferred_element_type=F32)


def tn(a, b):
    return lax.dot_general(a, b, (((0,), (0,)), ((), ())), preferred_element_type=F32)


def block_rows(c):
    return pl.ds(pl.multiple_of(c * C, C), C)


def lower_rows(m, s):
    return jnp.concatenate([m[a + s : a + 2 * s] for a in range(0, C, 2 * s)], 0)


def double(xs, offs, s):
    bs = [x.astype(BF16) for x in xs]
    if s < 16:
        rights = [nn(o, b).astype(BF16) for o, b in zip(offs, bs)]
        return [x - nn(b, r) for x, b, r in zip(xs, bs, rights)]
    rights = [nn(lower_rows(o, s), b).astype(BF16) for o, b in zip(offs, bs)]
    zero = jnp.zeros((s, C), BF16)
    count = C // (2 * s)
    fulls = [
        jnp.concatenate(sum([[zero, r[i * s : (i + 1) * s]] for i in range(count)], []), 0) for r in rights
    ]
    steps = [nn(lower_rows(b, s), f) for b, f in zip(bs, fulls)]
    return [
        jnp.concatenate(
            sum(
                [
                    [x[2 * i * s : (2 * i + 1) * s], x[(2 * i + 1) * s : (2 * i + 2) * s] - d[i * s : (i + 1) * s]]
                    for i in range(count)
                ],
                [],
            ),
            0,
        )
        for x, d in zip(xs, steps)
    ]


def kernel(
    q_hbm, k_hbm, v_hbm, g_hbm, b_hbm, gain_hbm, w_hbm, out_hbm,
    q_in, k_in, v_in, g_in, b_in, w_own, w_sib,
    q_f, k_f, v_f, g_f, b_f,
    q_send, k_send, v_send, g_send,
    q_recv, k_recv, v_recv, g_recv,
    masks, rk_row, rk_col, x_u, moves, wu, ku, before,
    y_q, y_o, gate,
    t_late, t_mine, l_mine, t_all, l_all, t_after, t_join, t_pre, l_pre, t_row, l_row, state, s_send, s_in,
    g_mine, g_sib, p_f, p_b, relay_a, relay_b, join_a, join_b,
    minus_a, minus_b, plus_a, plus_b,
    in_sem, own_sem, a2a_send, a2a_recv, w_send_sem, w_recv_sem,
    t_send, t_recv, l_send, l_recv, tr_send, tr_recv, lr_send, lr_recv, s_send_sem, s_recv,
    sib_send, sib_recv, rs_send, rs_recv, out_v, out_sem, gain_in,
):
    seq = lax.axis_index("seq")
    head = lax.axis_index("head")
    x = seq // NZ
    z = lax.rem(seq, NZ)
    y = head // 2
    core = lax.rem(head, 2)
    sibling = y * 2 + (1 - core)

    def on_head(h):
        return (seq, h)

    def on_z(zz):
        return (x * NZ + zz, head)

    def on_x(xx):
        return (xx * NZ + z, head)

    peers = [(0, 1), (3, 0), (3, 1), (1, 0), (1, 1), (2, 0), (2, 1)]

    def head_at(dy, dc):
        return lax.rem(y + dy, NY) * 2 + lax.rem(core + dc, 2)

    barrier = pltpu.get_barrier_semaphore()
    for dy, dc in peers:
        pl.semaphore_signal(barrier, inc=1, device_id=on_head(head_at(dy, dc)), device_id_type=MESH)
    for dz in range(1, NZ):
        pl.semaphore_signal(barrier, inc=1, device_id=on_z(lax.rem(z + dz, NZ)), device_id_type=MESH)
    for dx in range(1, NX):
        pl.semaphore_signal(barrier, inc=1, device_id=on_x(lax.rem(x + dx, NX)), device_id_type=MESH)

    loads = [
        pltpu.make_async_copy(src, dst, in_sem.at[i])
        for i, (src, dst) in enumerate(
            [(k_hbm, k_in), (b_hbm, b_in), (v_hbm, v_in), (q_hbm, q_in), (g_hbm, g_in), (w_hbm, w_own), (gain_hbm, gain_in)]
        )
    ]
    for copy in loads:
        copy.start()

    ri = lax.broadcasted_iota(jnp.int32, (C, C), 0)
    ci = lax.broadcasted_iota(jnp.int32, (C, C), 1)
    for i, s in enumerate(LEVELS):
        keep = (ri // (2 * s) == ci // (2 * s)) & (ri // s != ci // s)
        masks[i] = jnp.where(keep, 1.0, 0.0).astype(BF16)

    def to_columns(raw, wide, send, heads):
        per = heads // NH
        wide[...] = raw[...].astype(F32)
        for h in range(heads):
            send[h // per, :ROWS, (h % per) * C : (h % per + 1) * C] = wide[
                pl.ds(h, ROWS, stride=heads), :
            ].astype(BF16)

    sends = [(k_send, k_recv), (v_send, v_recv), (q_send, q_recv), (g_send, g_recv)]

    def peer_copy(array, i):
        send, recv = sends[array]
        target = head_at(*peers[i])
        return pltpu.make_async_remote_copy(
            src_ref=send.at[target],
            dst_ref=recv.at[head],
            send_sem=a2a_send.at[array, i],
            recv_sem=a2a_recv.at[array, i],
            device_id=on_head(target),
            device_id_type=MESH,
        )

    def own_copy(array):
        send, recv = sends[array]
        return pltpu.make_async_copy(send.at[head], recv.at[head], own_sem.at[array])

    def start_exchange(array):
        for i in range(len(peers)):
            peer_copy(array, i).start()
        own_copy(array).start()

    def wait_exchange(array):
        own_copy(array).wait()
        for i in range(len(peers)):
            peer_copy(array, i).wait_recv()

    def block(recv, c, cols):
        return jnp.concatenate([recv[2 * c + i, :ROWS, cols] for i in range(2)], 0)

    loads[0].wait()
    loads[1].wait()
    to_columns(k_in, k_f, k_send, HK * NH)
    lanes = lax.broadcasted_iota(jnp.int32, (ROWS, C), 1) - ROWS * lax.rem(head, 2)
    place = jnp.where(lanes == lax.broadcasted_iota(jnp.int32, (ROWS, C), 0), 1.0, 0.0).astype(BF16)
    b_f[: HV * NH, :] = nn(b_in[...], place)
    b_f[HV * NH :, :] = jnp.zeros((16, C), F32)
    for h in range(NH):
        k_send[h, ROWS:, :C] = b_f[h * HV : h * HV + 16, :].astype(BF16)
        k_send[h, ROWS:, C:] = jnp.zeros((16, C), BF16)
    pl.semaphore_wait(barrier, len(peers) + (NZ - 1) + (NX - 1))
    start_exchange(0)
    loads[2].wait()
    to_columns(v_in, v_f, v_send, HV * NH)
    loads[3].wait()
    to_columns(q_in, q_f, q_send, HK * NH)
    loads[4].wait()
    to_columns(g_in, g_f, g_send, HV * NH)
    for i in range(len(peers)):
        peer_copy(0, i).wait_send()
    start_exchange(1)
    weight_copy = pltpu.make_async_remote_copy(
        src_ref=w_hbm, dst_ref=w_sib, send_sem=w_send_sem, recv_sem=w_recv_sem,
        device_id=on_head(sibling), device_id_type=MESH,
    )

    eye = ri == ci

    def invert(blocks):
        todo = []
        for c in blocks:
            sums = sum(k_recv[2 * c + i, ROWS:, :C].astype(F32) for i in range(2))
            for j in range(HK):
                kb = block(k_recv, c, slice(j * C, (j + 1) * C))
                gram = nt(kb, kb)
                diag = jnp.where(eye, gram, 0.0)
                kc = lax.rsqrt(jnp.sum(diag, 1, keepdims=True) + EPS)
                kr = lax.rsqrt(jnp.sum(diag, 0, keepdims=True) + EPS)
                rk_row[j, c] = jnp.broadcast_to(kr, (8, C))
                rk_col[j, c] = jnp.broadcast_to(kc, (C, C))
                scaled = jnp.where(ri > ci, gram * kc * kr, 0.0)
                for n in (2 * j, 2 * j + 1):
                    br = sums[n : n + 1]
                    bc = jnp.sum(jnp.where(eye, br, 0.0), 1, keepdims=True)
                    a = scaled * bc
                    first = jnp.where(eye, 1.0, jnp.where(ri // 2 == ci // 2, -a, 0.0))
                    todo.append((n, c, a.astype(BF16), br, kr, kc, kb, first))
        xs = [t[-1] for t in todo]
        for i, s in enumerate(LEVELS):
            xs = double(xs, [t[2] * masks[i] for t in todo], s)
        ws = []
        for (n, c, _, br, kr, kc, kb, _), x in zip(todo, xs):
            right = x * br
            x_u[n, c] = right.astype(BF16)
            ws.append(nn((right * kr).astype(BF16), kb))
        for (n, c, _, br, kr, kc, kb, _), w in zip(todo, ws):
            wu[n, c, :, :C] = w.astype(BF16)
            moves[n, c] = tn(kb, (w * -kc).astype(BF16))

    def wait_keys(some):
        for i in some:
            peer_copy(0, i).wait_recv()

    own_copy(0).wait()
    wait_keys((0,))

    def halves(step, carry):
        @pl.when(step == 0)
        def _():
            wait_keys((1, 2))

        @pl.when(step == 1)
        def _():
            wait_keys((3, 4, 5, 6))

        invert((lax.rem(y + 3 * step, NY), lax.rem(y + 1 + step, NY)))
        return carry

    lax.fori_loop(0, 2, halves, 0)

    is_owner = lax.rem(z, 2) == core
    mine = z // 2

    def to_owner(mine_ref, all_ref, send, recv, n):
        return pltpu.make_async_remote_copy(
            src_ref=mine_ref.at[n], dst_ref=all_ref.at[z], send_sem=send.at[n], recv_sem=recv.at[z],
            device_id=on_z(2 * n + core), device_id_type=MESH,
        )

    def from_z(mine_ref, all_ref, send, recv, zz):
        return pltpu.make_async_remote_copy(
            src_ref=mine_ref.at[0], dst_ref=all_ref.at[zz], send_sem=send.at[0], recv_sem=recv.at[zz],
            device_id=on_z(zz), device_id_type=MESH,
        )

    t_refs = (t_mine, t_all, t_send, t_recv)
    l_refs = (l_mine, l_all, l_send, l_recv)

    def hand_in(refs):
        for n in range(HV):
            @pl.when(z != 2 * n + core)
            def _():
                to_owner(*refs, n).start()

            @pl.when(z == 2 * n + core)
            def _():
                refs[1][z] = refs[0][n]

    def gather(refs):
        for zz in range(NZ):
            @pl.when(z != zz)
            def _():
                from_z(*refs, zz).wait_recv()

    for n in range(HV):
        before[n, 0] = jnp.zeros((C, 2 * C), BF16)
    m_f = [[moves[n, c] for c in range(NB)] for n in range(HV)]
    m_b = [[m.astype(BF16) for m in ms] for ms in m_f]
    early = [(fs[0] + fs[1] + nn(bs[1], bs[0])).astype(BF16) for fs, bs in zip(m_f, m_b)]
    late = [fs[2] + fs[3] + nn(bs[3], bs[2]) for fs, bs in zip(m_f, m_b)]
    for n in range(HV):
        t_late[n] = late[n].astype(BF16)
    ts = [a.astype(F32) + b + nn(b.astype(BF16), a) for a, b in zip(early, late)]
    for n in range(HV):
        t_mine[n] = ts[n].astype(BF16)
    hand_in(t_refs)
    for n in range(HV):
        before[n, 1, :, :C] = m_b[n][0]
        before[n, 2, :, :C] = early[n]
        before[n, 3, :, :C] = (m_f[n][2] + early[n].astype(F32) + nn(m_b[n][2], early[n])).astype(BF16)

    wait_exchange(1)
    start_exchange(2)
    start_exchange(3)
    weight_copy.start()
    pair = 2

    def values(step, carry):
        todo = [(n, step * pair + i) for i in range(pair) for n in range(HV)]
        us = [nn(x_u[n, c], block(v_recv, c, slice(n * C, (n + 1) * C))) for n, c in todo]
        for (n, c), u in zip(todo, us):
            wu[n, c, :, C:] = u.astype(BF16)
        for (n, c), u in zip(todo, us):
            j = n // 2
            kb = block(k_recv, c, slice(j * C, (j + 1) * C))
            ku[n, c] = tn(kb, (u * rk_col[j, c]).astype(BF16))
        return carry

    lax.fori_loop(0, NB // pair, values, 0)
    first = [ku[n, 0].astype(BF16) for n in range(HV)]
    third = [ku[n, 2].astype(BF16) for n in range(HV)]
    early = [ku[n, 0] + ku[n, 1] + nn(moves[n, 1].astype(BF16), first[n]) for n in range(HV)]
    late = [ku[n, 2] + ku[n, 3] + nn(moves[n, 3].astype(BF16), third[n]) for n in range(HV)]
    early_b = [e.astype(BF16) for e in early]
    ls = [early[n] + late[n] + nn(t_late[n], early_b[n]) for n in range(HV)]
    for n in range(HV):
        l_mine[n] = ls[n].astype(BF16)
    hand_in(l_refs)
    for n in range(HV):
        before[n, 1, :, C:] = first[n]
        before[n, 2, :, C:] = early_b[n]
        before[n, 3, :, C:] = (ku[n, 2] + early[n] + nn(moves[n, 2].astype(BF16), early_b[n])).astype(BF16)

    assert NB == 4 and NZ == 8 and NX == 4
    tree = [
        [((1,), 0), ((3,), 2), ((5,), 4), ((7,), 6)],
        [((2, 3), 1), ((6, 7), 5)],
        [((4, 5, 6, 7), 3)],
    ]

    def to_x(row, send, recv, dx):
        return pltpu.make_async_remote_copy(
            src_ref=row.at[x], dst_ref=row.at[x], send_sem=send.at[dx], recv_sem=recv.at[x],
            device_id=on_x(x + dx), device_id_type=MESH,
        )

    def from_x(row, send, recv, xx):
        return pltpu.make_async_remote_copy(
            src_ref=row.at[xx], dst_ref=row.at[xx], send_sem=send.at[0], recv_sem=recv.at[xx],
            device_id=on_x(xx), device_id_type=MESH,
        )

    t_line = (t_row, tr_send, tr_recv)
    l_line = (l_row, lr_send, lr_recv)

    def to_z(zz):
        return pltpu.make_async_remote_copy(
            src_ref=s_send.at[zz], dst_ref=s_in.at[mine], send_sem=s_send_sem.at[zz], recv_sem=s_recv.at[mine],
            device_id=on_z(zz), device_id_type=MESH,
        )

    @pl.when(is_owner)
    def _():
        gather(t_refs)
        now = [t_all[zz] for zz in range(NZ)]
        for i, level in enumerate(tree):
            news = {}
            m = 0
            for laters, earlier in level:
                left = jnp.concatenate([now[later] for later in laters], 0)
                t_join[i, m * C : (m + len(laters)) * C] = left
                moved = nn(left, now[earlier])
                for a, later in enumerate(laters):
                    both = now[later].astype(F32) + now[earlier].astype(F32)
                    news[later] = (both + moved[a * C : (a + 1) * C]).astype(BF16)
                m += len(laters)
            for later in news:
                now[later] = news[later]
        for zz in range(NZ):
            t_pre[zz] = now[zz]

        def join(later, earlier):
            return (later.astype(F32) + earlier.astype(F32) + nn(later, earlier)).astype(BF16)

        all_t = [t_all[zz] for zz in range(NZ)]
        p32, p54 = t_join[1, C : 2 * C], t_join[2, C : 2 * C]
        p76, p74 = t_join[1, 3 * C :], t_join[2, 3 * C :]
        p21 = join(p32, all_t[1])
        for zz, value in [
            (0, join(p74, p21)), (1, join(p74, p32)), (2, join(p74, all_t[3])), (3, p74),
            (4, join(p76, all_t[5])), (5, p76), (6, all_t[7]),
        ]:
            t_after[:, zz * C : (zz + 1) * C] = value
        t_row[x] = now[NZ - 1]
        for dx in range(1, NX):
            @pl.when((x > 0) & (x + dx < NX))
            def _():
                to_x(*t_line, dx).start()

        gather(l_refs)
        lead = l_all[: NZ - 1].reshape((NZ - 1) * C, C)
        row = nn(t_after[...], lead)
        for zz in range(NZ):
            l_pre[zz] = l_all[zz].astype(F32)
            row = row + l_pre[zz]
        l_row[x] = row.astype(BF16)
        for dx in range(1, NX):
            @pl.when(x + dx < NX)
            def _():
                to_x(*l_line, dx).start()

        for i, level in enumerate(tree):
            m = 0
            for laters, earlier in level:
                first = l_pre[earlier]
                moved = nn(t_join[i, m * C : (m + len(laters)) * C], first.astype(BF16))
                for a, later in enumerate(laters):
                    l_pre[later] = l_pre[later] + first + moved[a * C : (a + 1) * C]
                m += len(laters)

        @pl.when(x == 0)
        def _():
            state[...] = jnp.zeros_like(state)

        @pl.when(x == 1)
        def _():
            from_x(*l_line, 0).wait_recv()
            state[...] = l_row[0].astype(F32)

        @pl.when(x == 2)
        def _():
            from_x(*t_line, 1).wait_recv()
            from_x(*l_line, 0).wait_recv()
            from_x(*l_line, 1).wait_recv()
            state[...] = nn(t_row[1], l_row[0]) + l_row[0].astype(F32) + l_row[1].astype(F32)

        @pl.when(x == 3)
        def _():
            from_x(*t_line, 1).wait_recv()
            from_x(*t_line, 2).wait_recv()
            both = join(t_row[2], t_row[1])
            for xx in range(NX - 1):
                from_x(*l_line, xx).wait_recv()
            state[...] = (
                nn(both, l_row[0]) + nn(t_row[2], l_row[1])
                + l_row[0].astype(F32) + l_row[1].astype(F32) + l_row[2].astype(F32)
            )

        start = state[...]
        start_b = start.astype(BF16)
        for zz in range(NZ):
            if zz == 0:
                s_send[zz] = start_b
            else:
                s_send[zz] = (start + nn(t_pre[zz - 1], start_b) + l_pre[zz - 1]).astype(BF16)

            @pl.when(z != zz)
            def _():
                to_z(zz).start()

            @pl.when(z == zz)
            def _():
                s_in[mine] = s_send[zz]

    wait_exchange(2)

    def outputs(c, carry):
        rows = block_rows(c)
        for j in range(HK):
            qb = block(q_recv, c, slice(j * C, (j + 1) * C))
            kb = block(k_recv, c, slice(j * C, (j + 1) * C))
            qf = qb.astype(F32)
            qc = lax.rsqrt(jnp.sum(qf * qf, 1, keepdims=True) + EPS) * (C ** -0.5)
            scores = jnp.where(ri >= ci, nt(qb, kb) * qc * rk_row[j, c, 0:1, :], 0.0).astype(BF16)
            unit = qf * qc
            for n in (2 * j, 2 * j + 1):
                part = nn(scores, wu[n, c])
                eff = unit - part[:, :C]
                moved = nn(eff.astype(BF16), before[n, c])
                y_q[n, rows, :] = (eff + moved[:, :C]).astype(BF16)
                y_o[n, rows, :] = part[:, C:] + moved[:, C:]
        return carry

    lax.fori_loop(0, NB, outputs, 0)

    wait_exchange(3)
    loads[6].wait()
    gain = gain_in[...].astype(F32)

    def gates(c, carry):
        rows = block_rows(c)
        for n in range(HV):
            v = block(g_recv, c, slice(n * C, (n + 1) * C)).astype(F32)
            gate[rows, n * C : (n + 1) * C] = v / (1.0 + jnp.exp(-v)) * gain
        return carry

    lax.fori_loop(0, NB, gates, 0)

    def to_sibling(n):
        cols = slice(n * C, (n + 1) * C)
        return pltpu.make_async_remote_copy(
            src_ref=g_mine.at[1 - core, :, cols], dst_ref=g_sib.at[:, cols],
            send_sem=sib_send.at[n], recv_sem=sib_recv.at[n],
            device_id=on_head(sibling), device_id_type=MESH,
        )

    for n in range(HV):
        @pl.when(z != 2 * n + core)
        def _():
            pltpu.make_async_remote_copy(
                src_ref=s_send.at[0], dst_ref=s_in.at[n], send_sem=s_send_sem.at[0], recv_sem=s_recv.at[n],
                device_id=on_z(2 * n + core), device_id_type=MESH,
            ).wait_recv()

        now = s_in[n]
        for c in range(NB):
            rows = slice(c * C, (c + 1) * C)
            values = nn(y_q[n, rows, :], now) + y_o[n, rows, :]
            spread = lax.rsqrt(jnp.mean(values * values, -1, keepdims=True) + EPS)
            gated = (values * spread * gate[rows, n * C : (n + 1) * C]).astype(BF16)
            for side in range(2):
                g_mine[side, c * ROWS : (c + 1) * ROWS, n * C : (n + 1) * C] = gated[
                    side * ROWS : (side + 1) * ROWS
                ]
        to_sibling(n).start()

    loads[5].wait()
    tile, piece = 256, 512

    def project(first, started):
        def one(t, carry):
            cols = pl.ds(pl.multiple_of(first + t * tile, tile), tile)
            value = p_f[:, cols] if started else nn(g_mine[core], w_own[:, cols])
            value = value + nn(g_sib[...], w_sib[:, cols])
            p_f[:, cols] = value
            p_b[:, cols] = value.astype(BF16)
            return carry

        lax.fori_loop(0, piece // tile, one, 0)

    def begin(first):
        def one(t, carry):
            cols = pl.ds(pl.multiple_of(first + t * tile, tile), tile)
            p_f[:, cols] = nn(g_mine[core], w_own[:, cols])
            return carry

        lax.fori_loop(0, piece // tile, one, 0)

    begin(0)
    begin(HALF)
    weight_copy.wait_recv()
    for n in range(HV):
        to_sibling(n).wait_recv()

    def rows_of(dy):
        return pl.ds(pl.multiple_of(lax.rem(y + dy, NY) * ROWS, ROWS), ROWS)

    def ring(i, src, dst, dy):
        return pltpu.make_async_remote_copy(
            src_ref=src, dst_ref=dst, send_sem=rs_send.at[i], recv_sem=rs_recv.at[i],
            device_id=on_head(lax.rem(y + dy, NY) * 2 + core), device_id_type=MESH,
        )

    a_cols, b_cols = slice(0, HALF), slice(HALF, DM)
    near = [slice(0, piece), slice(piece, HALF)]
    far = [slice(HALF, HALF + piece), slice(HALF + piece, DM)]
    relays_a = [ring(i, p_b.at[rows_of(2), near[i]], relay_a.at[:, near[i]], 1) for i in range(2)]
    relays_b = [ring(2 + i, p_b.at[rows_of(2), far[i]], relay_b.at[:, near[i]], 3) for i in range(2)]
    alone_a = ring(4, p_b.at[rows_of(3), a_cols], plus_a, 3)
    alone_b = ring(5, p_b.at[rows_of(1), b_cols], minus_b, 1)
    joins_a = [ring(6 + i, join_a.at[:, near[i]], minus_a.at[:, near[i]], 1) for i in range(2)]
    joins_b = [ring(8 + i, join_b.at[:, near[i]], plus_b.at[:, near[i]], 3) for i in range(2)]
    copies = relays_a + relays_b + [alone_a, alone_b] + joins_a + joins_b
    for i in range(2):
        project(i * piece, i == 0)
        relays_a[i].start()
        project(HALF + i * piece, i == 0)
        relays_b[i].start()
    alone_a.start()
    alone_b.start()
    for i in range(2):
        relays_a[i].wait_recv()
        join_a[:, near[i]] = (p_f[rows_of(1), near[i]] + relay_a[:, near[i]].astype(F32)).astype(BF16)
        joins_a[i].start()
        relays_b[i].wait_recv()
        join_b[:, near[i]] = (p_f[rows_of(3), far[i]] + relay_b[:, near[i]].astype(F32)).astype(BF16)
        joins_b[i].start()
    alone_a.wait_recv()
    alone_b.wait_recv()
    stores = []
    for i in range(2):
        for joins, cols, minus, plus in ((joins_a, near, minus_a, plus_a), (joins_b, far, minus_b, plus_b)):
            joins[i].wait_recv()
            out_v[:, cols[i]] = (
                p_f[rows_of(0), cols[i]] + minus[:, near[i]].astype(F32) + plus[:, near[i]].astype(F32)
            ).astype(BF16)
            store = pltpu.make_async_copy(
                out_v.at[:, cols[i]], out_hbm.at[:, cols[i]], out_sem.at[len(stores)]
            )
            store.start()
            stores.append(store)

    for array in range(1, 4):
        for i in range(len(peers)):
            peer_copy(array, i).wait_send()
    weight_copy.wait_send()
    for n in range(HV):
        to_sibling(n).wait_send()

        @pl.when(z != 2 * n + core)
        def _():
            to_owner(*t_refs, n).wait_send()
            to_owner(*l_refs, n).wait_send()

    @pl.when(is_owner)
    def _():
        for dx in range(1, NX):
            @pl.when((x > 0) & (x + dx < NX))
            def _():
                to_x(*t_line, dx).wait_send()

            @pl.when(x + dx < NX)
            def _():
                to_x(*l_line, dx).wait_send()

        for zz in range(NZ):
            @pl.when(z != zz)
            def _():
                to_z(zz).wait_send()

    for copy in copies:
        copy.wait_send()
    for store in stores:
        store.wait()


def per_device(queries, key_vectors, value_vectors, output_gate, write_strength, norm_gain, output_weight):
    any_space = pl.BlockSpec(memory_space=pl.ANY)
    dma = pltpu.SemaphoreType.DMA
    v = pltpu.VMEM
    kh, vh = HK * NH, HV * NH
    half = v((ROWS, HALF), BF16)
    scratch = [
        v((ROWS * kh, C), BF16), v((ROWS * kh, C), BF16), v((ROWS * vh, C), BF16), v((ROWS * vh, C), BF16),
        v((vh, ROWS), BF16), v((HV * C, DM), BF16), v((HV * C, DM), BF16),
        v((ROWS * kh, C), F32), v((ROWS * kh, C), F32), v((ROWS * vh, C), F32), v((ROWS * vh, C), F32), v((vh + 16, C), F32),
        v((NH, ROWS, HK * C), BF16), v((NH, KROWS, HK * C), BF16), v((NH, ROWS, HV * C), BF16), v((NH, ROWS, HV * C), BF16),
        v((NH, ROWS, HK * C), BF16), v((NH, KROWS, HK * C), BF16), v((NH, ROWS, HV * C), BF16), v((NH, ROWS, HV * C), BF16),
        v((len(LEVELS), C, C), BF16), v((HK, NB, 8, C), F32), v((HK, NB, C, C), F32),
        v((HV, NB, C, C), BF16), v((HV, NB, C, C), F32), v((HV, NB, C, 2 * C), BF16), v((HV, NB, C, C), F32),
        v((HV, NB, C, 2 * C), BF16),
        v((HV, TOK, C), BF16), v((HV, TOK, C), F32), v((TOK, HV * C), F32),
        v((HV, C, C), BF16), v((HV, C, C), BF16), v((HV, C, C), BF16), v((NZ, C, C), BF16), v((NZ, C, C), BF16),
        v((C, (NZ - 1) * C), BF16),
        v((3, 4 * C, C), BF16), v((NZ, C, C), BF16), v((NZ, C, C), F32), v((NX, C, C), BF16), v((NX, C, C), BF16),
        v((C, C), F32), v((NZ, C, C), BF16), v((HV, C, C), BF16),
        v((2, NY * ROWS, HV * C), BF16), v((NY * ROWS, HV * C), BF16),
        v((NY * ROWS, DM), F32), v((NY * ROWS, DM), BF16),
        half, half, half, half, half, half, half, half,
        dma((7,)), dma((4,)), dma((4, 7)), dma((4, 7)), dma, dma,
        dma((HV,)), dma((NZ,)), dma((HV,)), dma((NZ,)), dma((NX,)), dma((NX,)), dma((NX,)), dma((NX,)),
        dma((NZ,)), dma((HV,)),
        dma((HV,)), dma((HV,)), dma((10,)), dma((10,)), v((ROWS, DM), BF16), dma((4,)), v((1, C), BF16),
    ]
    return pl.pallas_call(
        kernel,
        out_shape=jax.ShapeDtypeStruct((ROWS, DM), BF16),
        in_specs=[any_space] * 7,
        out_specs=any_space,
        scratch_shapes=scratch,
        compiler_params=pltpu.CompilerParams(
            collective_id=0, has_side_effects=True, vmem_limit_bytes=60 * 1024 * 1024
        ),
    )(
        queries.reshape(ROWS * kh, C),
        key_vectors.reshape(ROWS * kh, C),
        value_vectors.reshape(ROWS * vh, C),
        output_gate.reshape(ROWS * vh, C),
        write_strength.T,
        norm_gain.reshape(1, C),
        output_weight,
    )


def solution(mesh):
    placed = (
        P(("seq", "head"), None, None),
        P(("seq", "head"), None, None),
        P(("seq", "head"), None, None),
        P(("seq", "head"), None, None),
        P(("seq", "head"), None),
        P(),
        P("head", None),
    )
    return jax.shard_map(
        per_device, mesh=mesh, in_specs=placed, out_specs=P(("seq", "head"), None), check_vma=False
    )
```

```python
import functools

import jax
import jax.numpy as jnp
from jax import lax
from jax.experimental import pallas as pl
from jax.experimental.pallas import tpu as pltpu
from jax.sharding import PartitionSpec as P

F32 = jnp.float32
BF16 = jnp.bfloat16
MESH = pl.DeviceIdType.MESH
EPS = 1e-06
C = 128
ROWS = 64
NH = 8
NZ = 8
NX = 4
NY = 4
HV = 4
HK = 2
TOK = ROWS * NH
NB = TOK // C
DM = 2048
HALF = DM // 2
LEVELS = (2, 4, 8, 16, 32, 64)
KROWS = ROWS + 16


def nn(a, b):
    return jnp.dot(a, b, preferred_element_type=F32)


def nt(a, b):
    return lax.dot_general(a, b, (((1,), (1,)), ((), ())), preferred_element_type=F32)


def tn(a, b):
    return lax.dot_general(a, b, (((0,), (0,)), ((), ())), preferred_element_type=F32)


def block_rows(c):
    return pl.ds(pl.multiple_of(c * C, C), C)


def lower_rows(m, s):
    return jnp.concatenate([m[a + s : a + 2 * s] for a in range(0, C, 2 * s)], 0)


def double(xs, offs, s):
    bs = [x.astype(BF16) for x in xs]
    if s < 16:
        rights = [nn(o, b).astype(BF16) for o, b in zip(offs, bs)]
        return [x - nn(b, r) for x, b, r in zip(xs, bs, rights)]
    rights = [nn(lower_rows(o, s), b).astype(BF16) for o, b in zip(offs, bs)]
    zero = jnp.zeros((s, C), BF16)
    count = C // (2 * s)
    fulls = [
        jnp.concatenate(sum([[zero, r[i * s : (i + 1) * s]] for i in range(count)], []), 0) for r in rights
    ]
    steps = [nn(lower_rows(b, s), f) for b, f in zip(bs, fulls)]
    return [
        jnp.concatenate(
            sum(
                [
                    [x[2 * i * s : (2 * i + 1) * s], x[(2 * i + 1) * s : (2 * i + 2) * s] - d[i * s : (i + 1) * s]]
                    for i in range(count)
                ],
                [],
            ),
            0,
        )
        for x, d in zip(xs, steps)
    ]


def kernel(
    q_hbm, k_hbm, v_hbm, g_hbm, b_hbm, gain_hbm, w_hbm, out_hbm,
    q_in, k_in, v_in, g_in, b_in, w_own, w_sib,
    q_f, k_f, v_f, g_f, b_f,
    q_send, k_send, v_send, g_send,
    q_recv, k_recv, v_recv, g_recv,
    masks, rk_row, rk_col, x_u, moves, wu, ku, before,
    y_q, y_o, gate,
    t_late, t_mine, l_mine, t_all, l_all, t_after, t_join, t_pre, l_pre, t_row, l_row, state, s_send, s_in,
    g_mine, g_sib, p_f, p_b, relay_a, relay_b, join_a, join_b,
    minus_a, minus_b, plus_a, plus_b,
    in_sem, own_sem, a2a_send, a2a_recv, w_send_sem, w_recv_sem,
    t_send, t_recv, l_send, l_recv, tr_send, tr_recv, lr_send, lr_recv, s_send_sem, s_recv,
    sib_send, sib_recv, rs_send, rs_recv, out_v, out_sem, gain_in,
):
    seq = lax.axis_index("seq")
    head = lax.axis_index("head")
    x = seq // NZ
    z = lax.rem(seq, NZ)
    y = head // 2
    core = lax.rem(head, 2)
    sibling = y * 2 + (1 - core)

    def on_head(h):
        return (seq, h)

    def on_z(zz):
        return (x * NZ + zz, head)

    def on_x(xx):
        return (xx * NZ + z, head)

    peers = [(0, 1), (3, 0), (3, 1), (1, 0), (1, 1), (2, 0), (2, 1)]

    def head_at(dy, dc):
        return lax.rem(y + dy, NY) * 2 + lax.rem(core + dc, 2)

    barrier = pltpu.get_barrier_semaphore()
    for dz in (4, 3, 5, 2, 6, 1, 7):
        pl.semaphore_signal(barrier, inc=1, device_id=on_z(lax.rem(z + dz, NZ)), device_id_type=MESH)
    for dx in range(1, NX):
        pl.semaphore_signal(barrier, inc=1, device_id=on_x(lax.rem(x + dx, NX)), device_id_type=MESH)

    for dy, dc in peers:
        pl.semaphore_signal(barrier, inc=1, device_id=on_head(head_at(dy, dc)), device_id_type=MESH)

    loads = [
        pltpu.make_async_copy(src, dst, in_sem.at[i])
        for i, (src, dst) in enumerate(
            [(k_hbm, k_in), (b_hbm, b_in), (v_hbm, v_in), (q_hbm, q_in), (g_hbm, g_in), (w_hbm, w_own), (gain_hbm, gain_in)]
        )
    ]
    for copy in loads:
        copy.start()

    ri = lax.broadcasted_iota(jnp.int32, (C, C), 0)
    ci = lax.broadcasted_iota(jnp.int32, (C, C), 1)
    for i, s in enumerate(LEVELS):
        keep = (ri // (2 * s) == ci // (2 * s)) & (ri // s != ci // s)
        masks[i] = jnp.where(keep, 1.0, 0.0).astype(BF16)

    def to_columns(raw, wide, send, heads):
        per = heads // NH
        wide[...] = raw[...].astype(F32)
        for h in range(heads):
            send[h // per, :ROWS, (h % per) * C : (h % per + 1) * C] = wide[
                pl.ds(h, ROWS, stride=heads), :
            ].astype(BF16)

    sends = [(k_send, k_recv), (v_send, v_recv), (q_send, q_recv), (g_send, g_recv)]

    def peer_copy(array, i):
        send, recv = sends[array]
        target = head_at(*peers[i])
        return pltpu.make_async_remote_copy(
            src_ref=send.at[target],
            dst_ref=recv.at[head],
            send_sem=a2a_send.at[array, i],
            recv_sem=a2a_recv.at[array, i],
            device_id=on_head(target),
            device_id_type=MESH,
        )

    def own_copy(array):
        send, recv = sends[array]
        return pltpu.make_async_copy(send.at[head], recv.at[head], own_sem.at[array])

    def start_exchange(array):
        for i in range(len(peers)):
            peer_copy(array, i).start()
        own_copy(array).start()

    def wait_exchange(array):
        own_copy(array).wait()
        for i in range(len(peers)):
            peer_copy(array, i).wait_recv()

    def block(recv, c, cols):
        return jnp.concatenate([recv[2 * c + i, :ROWS, cols] for i in range(2)], 0)

    loads[0].wait()
    loads[1].wait()
    to_columns(k_in, k_f, k_send, HK * NH)
    lanes = lax.broadcasted_iota(jnp.int32, (ROWS, C), 1) - ROWS * lax.rem(head, 2)
    place = jnp.where(lanes == lax.broadcasted_iota(jnp.int32, (ROWS, C), 0), 1.0, 0.0).astype(BF16)
    b_f[: HV * NH, :] = nn(b_in[...], place)
    b_f[HV * NH :, :] = jnp.zeros((16, C), F32)
    for h in range(NH):
        k_send[h, ROWS:, :C] = b_f[h * HV : h * HV + 16, :].astype(BF16)
        k_send[h, ROWS:, C:] = jnp.zeros((16, C), BF16)
    pl.semaphore_wait(barrier, len(peers) + (NZ - 1) + (NX - 1))
    start_exchange(0)
    loads[2].wait()
    to_columns(v_in, v_f, v_send, HV * NH)
    loads[3].wait()
    to_columns(q_in, q_f, q_send, HK * NH)
    loads[4].wait()
    to_columns(g_in, g_f, g_send, HV * NH)
    for i in range(len(peers)):
        peer_copy(0, i).wait_send()
    start_exchange(1)
    weight_copy = pltpu.make_async_remote_copy(
        src_ref=w_hbm, dst_ref=w_sib, send_sem=w_send_sem, recv_sem=w_recv_sem,
        device_id=on_head(sibling), device_id_type=MESH,
    )

    eye = ri == ci

    def invert(blocks):
        todo = []
        for c in blocks:
            sums = sum(k_recv[2 * c + i, ROWS:, :C].astype(F32) for i in range(2))
            for j in range(HK):
                kb = block(k_recv, c, slice(j * C, (j + 1) * C))
                gram = nt(kb, kb)
                diag = jnp.where(eye, gram, 0.0)
                kc = lax.rsqrt(jnp.sum(diag, 1, keepdims=True) + EPS)
                kr = lax.rsqrt(jnp.sum(diag, 0, keepdims=True) + EPS)
                rk_row[j, c] = jnp.broadcast_to(kr, (8, C))
                rk_col[j, c] = jnp.broadcast_to(kc, (C, C))
                scaled = jnp.where(ri > ci, gram * kc * kr, 0.0)
                for n in (2 * j, 2 * j + 1):
                    br = sums[n : n + 1]
                    bc = jnp.sum(jnp.where(eye, br, 0.0), 1, keepdims=True)
                    a = scaled * bc
                    first = jnp.where(eye, 1.0, jnp.where(ri // 2 == ci // 2, -a, 0.0))
                    todo.append((n, c, a.astype(BF16), br, kr, kc, kb, first))
        xs = [t[-1] for t in todo]
        for i, s in enumerate(LEVELS):
            xs = double(xs, [t[2] * masks[i] for t in todo], s)
        ws = []
        for (n, c, _, br, kr, kc, kb, _), x in zip(todo, xs):
            right = x * br
            x_u[n, c] = right.astype(BF16)
            ws.append(nn((right * kr).astype(BF16), kb))
        for (n, c, _, br, kr, kc, kb, _), w in zip(todo, ws):
            wu[n, c, :, :C] = w.astype(BF16)
            moves[n, c] = tn(kb, (w * -kc).astype(BF16))

    def wait_keys(some):
        for i in some:
            peer_copy(0, i).wait_recv()

    own_copy(0).wait()
    wait_keys((0,))

    def halves(step, carry):
        @pl.when(step == 0)
        def _():
            wait_keys((1, 2))

        @pl.when(step == 1)
        def _():
            wait_keys((3, 4, 5, 6))

        invert((lax.rem(y + 3 * step, NY), lax.rem(y + 1 + step, NY)))
        return carry

    lax.fori_loop(0, 2, halves, 0)

    is_owner = lax.rem(z, 2) == core
    mine = z // 2

    def to_owner(mine_ref, all_ref, send, recv, n):
        return pltpu.make_async_remote_copy(
            src_ref=mine_ref.at[n], dst_ref=all_ref.at[z], send_sem=send.at[n], recv_sem=recv.at[z],
            device_id=on_z(2 * n + core), device_id_type=MESH,
        )

    def from_z(mine_ref, all_ref, send, recv, zz):
        return pltpu.make_async_remote_copy(
            src_ref=mine_ref.at[0], dst_ref=all_ref.at[zz], send_sem=send.at[0], recv_sem=recv.at[zz],
            device_id=on_z(zz), device_id_type=MESH,
        )

    t_refs = (t_mine, t_all, t_send, t_recv)
    l_refs = (l_mine, l_all, l_send, l_recv)

    def hand_in(refs):
        for n in range(HV):
            @pl.when(z != 2 * n + core)
            def _():
                to_owner(*refs, n).start()

            @pl.when(z == 2 * n + core)
            def _():
                refs[1][z] = refs[0][n]

    def gather(refs):
        for zz in range(NZ):
            @pl.when(z != zz)
            def _():
                from_z(*refs, zz).wait_recv()

    for n in range(HV):
        before[n, 0] = jnp.zeros((C, 2 * C), BF16)
    m_f = [[moves[n, c] for c in range(NB)] for n in range(HV)]
    m_b = [[m.astype(BF16) for m in ms] for ms in m_f]
    early = [(fs[0] + fs[1] + nn(bs[1], bs[0])).astype(BF16) for fs, bs in zip(m_f, m_b)]
    late = [fs[2] + fs[3] + nn(bs[3], bs[2]) for fs, bs in zip(m_f, m_b)]
    for n in range(HV):
        t_late[n] = late[n].astype(BF16)
    ts = [a.astype(F32) + b + nn(b.astype(BF16), a) for a, b in zip(early, late)]
    for n in range(HV):
        t_mine[n] = ts[n].astype(BF16)
    hand_in(t_refs)
    for n in range(HV):
        before[n, 1, :, :C] = m_b[n][0]
        before[n, 2, :, :C] = early[n]
        before[n, 3, :, :C] = (m_f[n][2] + early[n].astype(F32) + nn(m_b[n][2], early[n])).astype(BF16)

    wait_exchange(1)
    start_exchange(2)
    start_exchange(3)
    weight_copy.start()
    pair = 2

    def values(step, carry):
        todo = [(n, step * pair + i) for i in range(pair) for n in range(HV)]
        us = [nn(x_u[n, c], block(v_recv, c, slice(n * C, (n + 1) * C))) for n, c in todo]
        for (n, c), u in zip(todo, us):
            wu[n, c, :, C:] = u.astype(BF16)
        for (n, c), u in zip(todo, us):
            j = n // 2
            kb = block(k_recv, c, slice(j * C, (j + 1) * C))
            ku[n, c] = tn(kb, (u * rk_col[j, c]).astype(BF16))
        return carry

    lax.fori_loop(0, NB // pair, values, 0)
    first = [ku[n, 0].astype(BF16) for n in range(HV)]
    third = [ku[n, 2].astype(BF16) for n in range(HV)]
    early = [ku[n, 0] + ku[n, 1] + nn(moves[n, 1].astype(BF16), first[n]) for n in range(HV)]
    late = [ku[n, 2] + ku[n, 3] + nn(moves[n, 3].astype(BF16), third[n]) for n in range(HV)]
    early_b = [e.astype(BF16) for e in early]
    ls = [early[n] + late[n] + nn(t_late[n], early_b[n]) for n in range(HV)]
    for n in range(HV):
        l_mine[n] = ls[n].astype(BF16)
    hand_in(l_refs)
    for n in range(HV):
        before[n, 1, :, C:] = first[n]
        before[n, 2, :, C:] = early_b[n]
        before[n, 3, :, C:] = (ku[n, 2] + early[n] + nn(moves[n, 2].astype(BF16), early_b[n])).astype(BF16)

    assert NB == 4 and NZ == 8 and NX == 4
    tree = [
        [((1,), 0), ((3,), 2), ((5,), 4), ((7,), 6)],
        [((2, 3), 1), ((6, 7), 5)],
        [((4, 5, 6, 7), 3)],
    ]

    def to_x(row, send, recv, dx):
        return pltpu.make_async_remote_copy(
            src_ref=row.at[x], dst_ref=row.at[x], send_sem=send.at[dx], recv_sem=recv.at[x],
            device_id=on_x(x + dx), device_id_type=MESH,
        )

    def from_x(row, send, recv, xx):
        return pltpu.make_async_remote_copy(
            src_ref=row.at[xx], dst_ref=row.at[xx], send_sem=send.at[0], recv_sem=recv.at[xx],
            device_id=on_x(xx), device_id_type=MESH,
        )

    t_line = (t_row, tr_send, tr_recv)
    l_line = (l_row, lr_send, lr_recv)

    def to_z(zz):
        return pltpu.make_async_remote_copy(
            src_ref=s_send.at[zz], dst_ref=s_in.at[mine], send_sem=s_send_sem.at[zz], recv_sem=s_recv.at[mine],
            device_id=on_z(zz), device_id_type=MESH,
        )

    @pl.when(is_owner)
    def _():
        gather(t_refs)
        now = [t_all[zz] for zz in range(NZ)]
        for i, level in enumerate(tree):
            news = {}
            m = 0
            for laters, earlier in level:
                left = jnp.concatenate([now[later] for later in laters], 0)
                t_join[i, m * C : (m + len(laters)) * C] = left
                moved = nn(left, now[earlier])
                for a, later in enumerate(laters):
                    both = now[later].astype(F32) + now[earlier].astype(F32)
                    news[later] = (both + moved[a * C : (a + 1) * C]).astype(BF16)
                m += len(laters)
            for later in news:
                now[later] = news[later]
        for zz in range(NZ):
            t_pre[zz] = now[zz]

        def join(later, earlier):
            return (later.astype(F32) + earlier.astype(F32) + nn(later, earlier)).astype(BF16)

        all_t = [t_all[zz] for zz in range(NZ)]
        p32, p54 = t_join[1, C : 2 * C], t_join[2, C : 2 * C]
        p76, p74 = t_join[1, 3 * C :], t_join[2, 3 * C :]
        p21 = join(p32, all_t[1])
        for zz, value in [
            (0, join(p74, p21)), (1, join(p74, p32)), (2, join(p74, all_t[3])), (3, p74),
            (4, join(p76, all_t[5])), (5, p76), (6, all_t[7]),
        ]:
            t_after[:, zz * C : (zz + 1) * C] = value
        t_row[x] = now[NZ - 1]
        for dx in range(1, NX):
            @pl.when((x > 0) & (x + dx < NX))
            def _():
                to_x(*t_line, dx).start()

        gather(l_refs)
        lead = l_all[: NZ - 1].reshape((NZ - 1) * C, C)
        row = nn(t_after[...], lead)
        for zz in range(NZ):
            l_pre[zz] = l_all[zz].astype(F32)
            row = row + l_pre[zz]
        l_row[x] = row.astype(BF16)
        for dx in range(1, NX):
            @pl.when(x + dx < NX)
            def _():
                to_x(*l_line, dx).start()

        for i, level in enumerate(tree):
            m = 0
            for laters, earlier in level:
                first = l_pre[earlier]
                moved = nn(t_join[i, m * C : (m + len(laters)) * C], first.astype(BF16))
                for a, later in enumerate(laters):
                    l_pre[later] = l_pre[later] + first + moved[a * C : (a + 1) * C]
                m += len(laters)

        @pl.when(x == 0)
        def _():
            state[...] = jnp.zeros_like(state)

        @pl.when(x == 1)
        def _():
            from_x(*l_line, 0).wait_recv()
            state[...] = l_row[0].astype(F32)

        @pl.when(x == 2)
        def _():
            from_x(*t_line, 1).wait_recv()
            from_x(*l_line, 0).wait_recv()
            from_x(*l_line, 1).wait_recv()
            state[...] = nn(t_row[1], l_row[0]) + l_row[0].astype(F32) + l_row[1].astype(F32)

        @pl.when(x == 3)
        def _():
            from_x(*t_line, 1).wait_recv()
            from_x(*t_line, 2).wait_recv()
            both = join(t_row[2], t_row[1])
            for xx in range(NX - 1):
                from_x(*l_line, xx).wait_recv()
            state[...] = (
                nn(both, l_row[0]) + nn(t_row[2], l_row[1])
                + l_row[0].astype(F32) + l_row[1].astype(F32) + l_row[2].astype(F32)
            )

        start = state[...]
        start_b = start.astype(BF16)
        for zz in range(NZ):
            if zz == 0:
                s_send[zz] = start_b
            else:
                s_send[zz] = (start + nn(t_pre[zz - 1], start_b) + l_pre[zz - 1]).astype(BF16)

            @pl.when(z != zz)
            def _():
                to_z(zz).start()

            @pl.when(z == zz)
            def _():
                s_in[mine] = s_send[zz]

    wait_exchange(2)

    def outputs(c, carry):
        rows = block_rows(c)
        for j in range(HK):
            qb = block(q_recv, c, slice(j * C, (j + 1) * C))
            kb = block(k_recv, c, slice(j * C, (j + 1) * C))
            qf = qb.astype(F32)
            qc = lax.rsqrt(jnp.sum(qf * qf, 1, keepdims=True) + EPS) * (C ** -0.5)
            scores = jnp.where(ri >= ci, nt(qb, kb) * qc * rk_row[j, c, 0:1, :], 0.0).astype(BF16)
            unit = qf * qc
            for n in (2 * j, 2 * j + 1):
                part = nn(scores, wu[n, c])
                eff = unit - part[:, :C]
                moved = nn(eff.astype(BF16), before[n, c])
                y_q[n, rows, :] = (eff + moved[:, :C]).astype(BF16)
                y_o[n, rows, :] = part[:, C:] + moved[:, C:]
        return carry

    lax.fori_loop(0, NB, outputs, 0)

    wait_exchange(3)
    loads[6].wait()
    gain = gain_in[...].astype(F32)

    def gates(c, carry):
        rows = block_rows(c)
        for n in range(HV):
            v = block(g_recv, c, slice(n * C, (n + 1) * C)).astype(F32)
            gate[rows, n * C : (n + 1) * C] = v / (1.0 + jnp.exp(-v)) * gain
        return carry

    lax.fori_loop(0, NB, gates, 0)

    def to_sibling(n):
        cols = slice(n * C, (n + 1) * C)
        return pltpu.make_async_remote_copy(
            src_ref=g_mine.at[1 - core, :, cols], dst_ref=g_sib.at[:, cols],
            send_sem=sib_send.at[n], recv_sem=sib_recv.at[n],
            device_id=on_head(sibling), device_id_type=MESH,
        )

    for n in range(HV):
        @pl.when(z != 2 * n + core)
        def _():
            pltpu.make_async_remote_copy(
                src_ref=s_send.at[0], dst_ref=s_in.at[n], send_sem=s_send_sem.at[0], recv_sem=s_recv.at[n],
                device_id=on_z(2 * n + core), device_id_type=MESH,
            ).wait_recv()

        now = s_in[n]
        for c in range(NB):
            rows = slice(c * C, (c + 1) * C)
            values = nn(y_q[n, rows, :], now) + y_o[n, rows, :]
            spread = lax.rsqrt(jnp.mean(values * values, -1, keepdims=True) + EPS)
            gated = (values * spread * gate[rows, n * C : (n + 1) * C]).astype(BF16)
            for side in range(2):
                g_mine[side, c * ROWS : (c + 1) * ROWS, n * C : (n + 1) * C] = gated[
                    side * ROWS : (side + 1) * ROWS
                ]
        to_sibling(n).start()

    loads[5].wait()
    tile, piece = 256, 512

    def project(first, started):
        def one(t, carry):
            cols = pl.ds(pl.multiple_of(first + t * tile, tile), tile)
            value = p_f[:, cols] if started else nn(g_mine[core], w_own[:, cols])
            value = value + nn(g_sib[...], w_sib[:, cols])
            p_f[:, cols] = value
            p_b[:, cols] = value.astype(BF16)
            return carry

        lax.fori_loop(0, piece // tile, one, 0)

    def begin(first):
        def one(t, carry):
            cols = pl.ds(pl.multiple_of(first + t * tile, tile), tile)
            p_f[:, cols] = nn(g_mine[core], w_own[:, cols])
            return carry

        lax.fori_loop(0, piece // tile, one, 0)

    begin(0)
    begin(HALF)
    weight_copy.wait_recv()
    for n in range(HV):
        to_sibling(n).wait_recv()

    def rows_of(dy):
        return pl.ds(pl.multiple_of(lax.rem(y + dy, NY) * ROWS, ROWS), ROWS)

    def ring(i, src, dst, dy):
        return pltpu.make_async_remote_copy(
            src_ref=src, dst_ref=dst, send_sem=rs_send.at[i], recv_sem=rs_recv.at[i],
            device_id=on_head(lax.rem(y + dy, NY) * 2 + core), device_id_type=MESH,
        )

    a_cols, b_cols = slice(0, HALF), slice(HALF, DM)
    near = [slice(0, piece), slice(piece, HALF)]
    far = [slice(HALF, HALF + piece), slice(HALF + piece, DM)]
    relays_a = [ring(i, p_b.at[rows_of(2), near[i]], relay_a.at[:, near[i]], 1) for i in range(2)]
    relays_b = [ring(2 + i, p_b.at[rows_of(2), far[i]], relay_b.at[:, near[i]], 3) for i in range(2)]
    alone_a = ring(4, p_b.at[rows_of(3), a_cols], plus_a, 3)
    alone_b = ring(5, p_b.at[rows_of(1), b_cols], minus_b, 1)
    joins_a = [ring(6 + i, join_a.at[:, near[i]], minus_a.at[:, near[i]], 1) for i in range(2)]
    joins_b = [ring(8 + i, join_b.at[:, near[i]], plus_b.at[:, near[i]], 3) for i in range(2)]
    copies = relays_a + relays_b + [alone_a, alone_b] + joins_a + joins_b
    for i in range(2):
        project(i * piece, i == 0)
        relays_a[i].start()
        project(HALF + i * piece, i == 0)
        relays_b[i].start()
    alone_a.start()
    alone_b.start()
    for i in range(2):
        relays_a[i].wait_recv()
        join_a[:, near[i]] = (p_f[rows_of(1), near[i]] + relay_a[:, near[i]].astype(F32)).astype(BF16)
        joins_a[i].start()
        relays_b[i].wait_recv()
        join_b[:, near[i]] = (p_f[rows_of(3), far[i]] + relay_b[:, near[i]].astype(F32)).astype(BF16)
        joins_b[i].start()
    alone_a.wait_recv()
    alone_b.wait_recv()
    stores = []
    for i in range(2):
        for joins, cols, minus, plus in ((joins_a, near, minus_a, plus_a), (joins_b, far, minus_b, plus_b)):
            joins[i].wait_recv()
            out_v[:, cols[i]] = (
                p_f[rows_of(0), cols[i]] + minus[:, near[i]].astype(F32) + plus[:, near[i]].astype(F32)
            ).astype(BF16)
            store = pltpu.make_async_copy(
                out_v.at[:, cols[i]], out_hbm.at[:, cols[i]], out_sem.at[len(stores)]
            )
            store.start()
            stores.append(store)

    for array in range(1, 4):
        for i in range(len(peers)):
            peer_copy(array, i).wait_send()
    weight_copy.wait_send()
    for n in range(HV):
        to_sibling(n).wait_send()

        @pl.when(z != 2 * n + core)
        def _():
            to_owner(*t_refs, n).wait_send()
            to_owner(*l_refs, n).wait_send()

    @pl.when(is_owner)
    def _():
        for dx in range(1, NX):
            @pl.when((x > 0) & (x + dx < NX))
            def _():
                to_x(*t_line, dx).wait_send()

            @pl.when(x + dx < NX)
            def _():
                to_x(*l_line, dx).wait_send()

        for zz in range(NZ):
            @pl.when(z != zz)
            def _():
                to_z(zz).wait_send()

    for copy in copies:
        copy.wait_send()
    for store in stores:
        store.wait()


def per_device(queries, key_vectors, value_vectors, output_gate, write_strength, norm_gain, output_weight):
    any_space = pl.BlockSpec(memory_space=pl.ANY)
    dma = pltpu.SemaphoreType.DMA
    v = pltpu.VMEM
    kh, vh = HK * NH, HV * NH
    half = v((ROWS, HALF), BF16)
    scratch = [
        v((ROWS * kh, C), BF16), v((ROWS * kh, C), BF16), v((ROWS * vh, C), BF16), v((ROWS * vh, C), BF16),
        v((vh, ROWS), BF16), v((HV * C, DM), BF16), v((HV * C, DM), BF16),
        v((ROWS * kh, C), F32), v((ROWS * kh, C), F32), v((ROWS * vh, C), F32), v((ROWS * vh, C), F32), v((vh + 16, C), F32),
        v((NH, ROWS, HK * C), BF16), v((NH, KROWS, HK * C), BF16), v((NH, ROWS, HV * C), BF16), v((NH, ROWS, HV * C), BF16),
        v((NH, ROWS, HK * C), BF16), v((NH, KROWS, HK * C), BF16), v((NH, ROWS, HV * C), BF16), v((NH, ROWS, HV * C), BF16),
        v((len(LEVELS), C, C), BF16), v((HK, NB, 8, C), F32), v((HK, NB, C, C), F32),
        v((HV, NB, C, C), BF16), v((HV, NB, C, C), F32), v((HV, NB, C, 2 * C), BF16), v((HV, NB, C, C), F32),
        v((HV, NB, C, 2 * C), BF16),
        v((HV, TOK, C), BF16), v((HV, TOK, C), F32), v((TOK, HV * C), F32),
        v((HV, C, C), BF16), v((HV, C, C), BF16), v((HV, C, C), BF16), v((NZ, C, C), BF16), v((NZ, C, C), BF16),
        v((C, (NZ - 1) * C), BF16),
        v((3, 4 * C, C), BF16), v((NZ, C, C), BF16), v((NZ, C, C), F32), v((NX, C, C), BF16), v((NX, C, C), BF16),
        v((C, C), F32), v((NZ, C, C), BF16), v((HV, C, C), BF16),
        v((2, NY * ROWS, HV * C), BF16), v((NY * ROWS, HV * C), BF16),
        v((NY * ROWS, DM), F32), v((NY * ROWS, DM), BF16),
        half, half, half, half, half, half, half, half,
        dma((7,)), dma((4,)), dma((4, 7)), dma((4, 7)), dma, dma,
        dma((HV,)), dma((NZ,)), dma((HV,)), dma((NZ,)), dma((NX,)), dma((NX,)), dma((NX,)), dma((NX,)),
        dma((NZ,)), dma((HV,)),
        dma((HV,)), dma((HV,)), dma((10,)), dma((10,)), v((ROWS, DM), BF16), dma((4,)), v((1, C), BF16),
    ]
    return pl.pallas_call(
        kernel,
        out_shape=jax.ShapeDtypeStruct((ROWS, DM), BF16),
        in_specs=[any_space] * 7,
        out_specs=any_space,
        scratch_shapes=scratch,
        compiler_params=pltpu.CompilerParams(
            collective_id=0, has_side_effects=True, vmem_limit_bytes=60 * 1024 * 1024
        ),
    )(
        queries.reshape(ROWS * kh, C),
        key_vectors.reshape(ROWS * kh, C),
        value_vectors.reshape(ROWS * vh, C),
        output_gate.reshape(ROWS * vh, C),
        write_strength.T,
        norm_gain.reshape(1, C),
        output_weight,
    )


def solution(mesh):
    placed = (
        P(("seq", "head"), None, None),
        P(("seq", "head"), None, None),
        P(("seq", "head"), None, None),
        P(("seq", "head"), None, None),
        P(("seq", "head"), None),
        P(),
        P("head", None),
    )
    return jax.shard_map(
        per_device, mesh=mesh, in_specs=placed, out_specs=P(("seq", "head"), None), check_vma=False
    )
```
